32 devices in a mesh: dp: 16 (over z, x, core), tensor: 2 (over y).
Axes of the slice: x: 2, y: 2, z: 4, core: 2. Of those that a mesh axis runs over, the one named last changes fastest.
Arguments:
- tokens: bfloat16 [8192, 2048], P(('dp', 'tensor')), may hold values from -6 to 6
- lengths: int32 [16, 2], P('dp'), may hold values from 0 to 512, as said below
- w_qkv: bfloat16 [2048, 8, 768], P('dp', 'tensor'), may hold values from -0.125 to 0.125
- b_qkv: float32 [8, 768], P('tensor'), may hold values from -2 to 2
- w_out: bfloat16 [2048, 8, 256], P('dp', 'tensor'), may hold values from -0.75 to 0.75
- b_out: float32 [2048], replicated, may hold values from -2 to 2
- w_fc: bfloat16 [2048, 8192], P('dp', 'tensor'), may hold values from -0.125 to 0.125
- b_fc: float32 [8192], P('tensor'), may hold values from -2 to 2
- w_proj: bfloat16 [2048, 8192], P('dp', 'tensor'), may hold values from -0.0625 to 0.0625
- b_proj: float32 [2048], replicated, may hold values from -2 to 2
- gain_attn: float32 [2048], replicated, may hold values from 0.5 to 1.5
- shift_attn: float32 [2048], replicated, may hold values from -2 to 2
- gain_mlp: float32 [2048], replicated, may hold values from 0.5 to 1.5
- shift_mlp: float32 [2048], replicated, may hold values from -2 to 2
- cotangent: bfloat16 [8192, 2048], P(('dp', 'tensor')), may hold values from -6 to 6
Outputs:
- output: bfloat16 [8192, 2048], P(('dp', 'tensor'))
- grad_tokens: bfloat16 [8192, 2048], P(('dp', 'tensor'))
- grad_w_qkv: float32 [2048, 8, 768], P('dp', 'tensor')
- grad_b_qkv: float32 [8, 768], P('tensor')
- grad_w_out: float32 [2048, 8, 256], P('dp', 'tensor')
- grad_b_out: float32 [2048], replicated
- grad_w_fc: float32 [2048, 8192], P('dp', 'tensor')
- grad_b_fc: float32 [8192], P('tensor')
- grad_w_proj: float32 [2048, 8192], P('dp', 'tensor')
- grad_b_proj: float32 [2048], replicated
- grad_gain_attn: float32 [2048], replicated
- grad_shift_attn: float32 [2048], replicated
- grad_gain_mlp: float32 [2048], replicated
- grad_shift_mlp: float32 [2048], replicated
The draws below stay inside these ranges and needn't reach their ends.
Inputs may be any that keep to these rules, and one draw needn't show every extreme that they name: Row g holds the lengths of the two sequences packed from the first row of data group g; the first is longer than 256, both together are at most 512, the remaining rows are padding, and in one group drawn from the seed the first sequence fills all 512 rows.
All inputs are finite; a program needn't handle non-finite values.
Results may differ from the reference program's by a relative error of at most 0.011.
Values may be sent and summed in bfloat16 or wider, within the bound.
A program may use at most 256 MiB of HBM per device.

```python
import math
import jax
import jax.numpy as jnp
from jax import lax

D = 2048
HEADS = 8
HEAD = 256
ROT = 64
FF = 8192
CAP = 512
TOKENS = 8192
N_DP = 16


def draw_lengths(key, part):
    key = jax.random.fold_in(key, 11)
    first_key, second_key, whole_key = jax.random.split(key, 3)
    first_len = jax.random.randint(first_key, (N_DP,), CAP // 2 + 1, CAP + 1)
    second_len = jax.random.randint(second_key, (N_DP,), 0, CAP - first_len + 1)
    whole_group = jax.random.randint(whole_key, (), 0, N_DP)
    chosen = jnp.arange(N_DP) == whole_group
    first_len = jnp.where(chosen, CAP, first_len)
    second_len = jnp.where(chosen, 0, second_len)
    return jnp.stack([first_len, second_len], axis=1).astype(jnp.int32)


def with_spikes(entries, stream_key, source, target, shards_of, factor):
    owner, partner = [(jnp.arange(entries.shape[dim]) // (entries.shape[dim] // shards_of)).reshape([-1 if axis == dim else 1 for axis in range(entries.ndim)]) for dim in (source, target)]
    chosen = jax.random.permutation(stream_key, shards_of)[partner]
    strong = (owner == chosen) | (owner == (partner + shards_of // 2) % shards_of)
    return jnp.where(strong, factor * entries, entries)


def steps_of(rng, extent, cuts, smallest, high):
    gain = 1.0
    for axis_at, parts in cuts:
        draws = jax.random.uniform(jax.random.fold_in(jax.random.fold_in(rng, 6), axis_at), (parts,), jnp.float32, smallest / len(cuts), high / len(cuts))
        gain = gain * jnp.repeat(jnp.exp(draws), extent[axis_at] // parts).reshape((-1,) + (1,) * (len(extent) - 1 - axis_at))
    return gain


def noise(rng, extent, width, reach, cuts=(), held_as=jnp.bfloat16):
    drawn = jax.random.normal(rng, extent, jnp.float32) * width
    if len(cuts) > 0:
        drawn = steps_of(rng, extent, cuts, -0.22, 0.18) * drawn
    return jnp.clip(drawn, min=-reach, max=reach).astype(held_as)


def heavy_noise(own_key, extent, deviation, limit, cuts, heavy, kind=jnp.bfloat16):
    drawn = deviation * jax.random.normal(own_key, extent, jnp.float32)
    if cuts:
        drawn = drawn * steps_of(own_key, extent, cuts, -0.22, 0.18)
    return jnp.clip(with_spikes(drawn, jax.random.fold_in(own_key, 3), *heavy), -limit, limit).astype(kind)


def setup_inputs(seed: int = 0) -> dict:
    keys = jax.random.split(jax.random.key(seed), 16)
    return {
        "tokens": noise(keys[0], (TOKENS, D), 1.0, 6.0, ((0, 32),)),
        "lengths": draw_lengths(jax.random.fold_in(keys[15], 71), 0),
        "w_qkv": noise(keys[2], (D, HEADS, 3 * HEAD), D ** -0.5, 0.125, ((0, 16), (1, 2))),
        "b_qkv": noise(keys[3], (HEADS, 3 * HEAD), 0.3, 2.0, ((0, 2),), jnp.float32),
        "w_out": noise(keys[4], (D, HEADS, HEAD), (D // 32) ** -0.5, 0.75, ((0, 16), (1, 2))),
        "b_out": noise(keys[5], (D,), 0.3, 2.0, (), jnp.float32),
        "w_fc": noise(keys[6], (D, FF), D ** -0.5, 0.125, ((0, 16), (1, 2))),
        "b_fc": noise(keys[7], (FF,), 0.3, 2.0, ((0, 2),), jnp.float32),
        "w_proj": noise(keys[8], (D, FF), FF ** -0.5, 0.0625, ((0, 16), (1, 2))),
        "b_proj": noise(keys[9], (D,), 0.3, 2.0, (), jnp.float32),
        "gain_attn": jnp.clip(1.0 + 0.1 * jax.random.normal(keys[10], (D,), jnp.float32), 0.5, 1.5),
        "shift_attn": noise(keys[11], (D,), 0.3, 2.0, (), jnp.float32),
        "gain_mlp": jnp.clip(1.0 + 0.1 * jax.random.normal(keys[12], (D,), jnp.float32), 0.5, 1.5),
        "shift_mlp": noise(keys[13], (D,), 0.3, 2.0, (), jnp.float32),
        "cotangent": heavy_noise(keys[14], (TOKENS, D), 1.0, 6.0, ((0, 32),), (0, 1, 32, 2.75)),
    }


@jax.custom_vjp
def low(v):
    return lax.optimization_barrier(v.astype(jnp.bfloat16)).astype(jnp.float32)

@jax.custom_vjp
def low_back(v):
    return v

def low_keep(v):
    return (low(v), None)

def low_pass(kept, grad):
    return (grad,)

def back_keep(v):
    return (v, None)

def back_low(kept, grad):
    return (low(grad),)
low.defvjp(low_keep, low_pass)
low_back.defvjp(back_keep, back_low)
HIGHEST = lax.Precision.HIGHEST

def layout(length_row, row_index):
    first_len = length_row[0]
    both_len = first_len + length_row[1]
    segment = (row_index >= first_len).astype(jnp.int32) + (row_index >= both_len).astype(jnp.int32)
    begin = jnp.where(segment == 0, 0, jnp.where(segment == 1, first_len, both_len))
    return (segment, (row_index - begin).astype(jnp.float32))

def angles(position):
    freq_index = jnp.arange(ROT // 2, dtype=jnp.float32) * (2.0 / ROT)
    inverse = jnp.exp(freq_index * -math.log(10000.0))
    phase_angle = position[:, None] * inverse[None, :]
    return (jnp.cos(phase_angle)[:, None, :], jnp.sin(phase_angle)[:, None, :])

def rotary(vector, cosine, sine_part):
    half_rot = ROT // 2
    lower_part = vector[..., :half_rot]
    upper_part = vector[..., half_rot:ROT]
    return jnp.concatenate([lower_part * cosine - upper_part * sine_part, upper_part * cosine + lower_part * sine_part, vector[..., ROT:]], axis=-1)

def layer_norm(vector, gain_vec, shift_vec):
    center = vector - lax.optimization_barrier(jnp.mean(vector, axis=-1, keepdims=True))
    spread = lax.optimization_barrier(jnp.mean(center * center, axis=-1, keepdims=True))
    return center * lax.rsqrt(spread + 1e-05) * gain_vec + shift_vec

def group_forward(params, inputs, length_row):
    w_qkv, b_qkv, w_out, b_out, w_fc, b_fc, w_proj, b_proj, gain_attn, shift_attn, gain_mlp, shift_mlp = params
    row_index = jnp.arange(CAP, dtype=jnp.int32)
    segment, position = layout(length_row, row_index)
    live_rows = (segment < 2).astype(inputs.dtype)[:, None]
    cosine, sine_part = angles(position)
    normed_attn = low(layer_norm(inputs, gain_attn, shift_attn))
    normed_mlp = low(layer_norm(inputs, gain_mlp, shift_mlp))
    joined_qkv = low_back(jnp.einsum('td,dhe->the', normed_attn, w_qkv, precision=HIGHEST) + b_qkv)
    queries = low(rotary(joined_qkv[..., :HEAD], cosine, sine_part))
    key_rot = low(rotary(joined_qkv[..., HEAD:2 * HEAD], cosine, sine_part))
    values = low(joined_qkv[..., 2 * HEAD:])
    scores = low_back(jnp.einsum('qhe,khe->hqk', queries, key_rot, precision=HIGHEST) * (1.0 / math.sqrt(HEAD)))
    allowed = (segment[:, None] == segment[None, :]) & (row_index[:, None] >= row_index[None, :])
    scores = jnp.where(allowed[None], scores, -1e+30)
    shifted = jnp.exp(scores - lax.optimization_barrier(jnp.max(scores, axis=-1, keepdims=True)))
    attn_probs = low(shifted / lax.optimization_barrier(jnp.sum(shifted, axis=-1, keepdims=True)))
    mixed_heads = low(low_back(jnp.einsum('hqk,khe->qhe', attn_probs, values, precision=HIGHEST)))
    attended = jnp.einsum('qhe,dhe->qd', mixed_heads, w_out, precision=HIGHEST)
    hidden_pre = low_back(jnp.dot(normed_mlp, w_fc, precision=HIGHEST) + b_fc)
    hidden = low(jax.nn.gelu(hidden_pre, approximate=False))
    projected = jnp.einsum('tf,df->td', hidden, w_proj, precision=HIGHEST)
    return inputs + live_rows * (attended + projected + b_out + b_proj)

def reference(tokens, lengths, w_qkv, b_qkv, w_out, b_out, w_fc, b_fc, w_proj, b_proj, gain_attn, shift_attn, gain_mlp, shift_mlp, cotangent):
    params = tuple((weight_item.astype(jnp.float32) for weight_item in (w_qkv, b_qkv, w_out, b_out, w_fc, b_fc, w_proj, b_proj, gain_attn, shift_attn, gain_mlp, shift_mlp)))
    inputs = tokens.astype(jnp.float32).reshape(N_DP, CAP, D)
    step_fn = jax.checkpoint(group_forward)

    def forward(weights_all, resid_all):
        return lax.map(lambda carried: step_fn(weights_all, carried[0], carried[1]), (resid_all, lengths))
    result, pullback = jax.vjp(forward, params, inputs)
    grad_params, grad_inputs = pullback(cotangent.astype(jnp.float32).reshape(N_DP, CAP, D))
    return (result.reshape(TOKENS, D).astype(jnp.bfloat16), grad_inputs.reshape(TOKENS, D).astype(jnp.bfloat16), grad_params[0], grad_params[1], grad_params[2], grad_params[3], grad_params[4], grad_params[5], grad_params[6], grad_params[7], grad_params[8], grad_params[9], grad_params[10], grad_params[11])
```

```python
import math

import jax
import jax.numpy as jnp
from jax import lax
from jax.sharding import Mesh
from jax.sharding import PartitionSpec as P

HEAD = 256
ROT = 64
INNER = 4
CHUNKS = 4
F32 = jnp.float32
BF16 = jnp.bfloat16


def layout(length_row, row_index):
    first_len = length_row[0]
    both_len = first_len + length_row[1]
    segment = (row_index >= first_len).astype(jnp.int32) + (row_index >= both_len).astype(jnp.int32)
    begin = jnp.where(segment == 0, 0, jnp.where(segment == 1, first_len, both_len))
    return (segment, (row_index - begin).astype(F32))


def angles(position):
    freq_index = jnp.arange(ROT // 2, dtype=F32) * (2.0 / ROT)
    inverse = jnp.exp(freq_index * -math.log(10000.0))
    phase_angle = position[..., None] * inverse
    return (jnp.cos(phase_angle), jnp.sin(phase_angle))


def rotary(vector, cosine, sine_part):
    half_rot = ROT // 2
    lower_part = vector[..., :half_rot]
    upper_part = vector[..., half_rot:ROT]
    return jnp.concatenate(
        [
            lower_part * cosine - upper_part * sine_part,
            upper_part * cosine + lower_part * sine_part,
            vector[..., ROT:],
        ],
        axis=-1,
    )


def norm_stats(residual):
    center = residual - jnp.mean(residual, axis=-1, keepdims=True)
    spread = jnp.mean(center * center, axis=-1, keepdims=True)
    inv_dev = lax.rsqrt(spread + 1e-05)
    return center * inv_dev, inv_dev


def gelu_slope(vector):
    return 0.5 * (1.0 + lax.erf(vector * (1.0 / math.sqrt(2.0)))) + vector * jnp.exp(
        -0.5 * vector * vector
    ) * (1.0 / math.sqrt(2.0 * math.pi))


def dot(a, b, dims):
    return lax.dot_general(a, b, (dims, ((), ())), preferred_element_type=F32)


NN = ((1,), (0,))
NT = ((1,), (1,))
TN = ((0,), (0,))


def line_gather(shard, z, n):
    up = [shard]
    down = [shard]
    for s in range(1, n):
        up.append(lax.ppermute(up[-1], "outer", [(i, i + 1) for i in range(s - 1, n - 1)]))
        down.append(lax.ppermute(down[-1], "outer", [(i, i - 1) for i in range(1, n - s + 1)]))
    slots = [shard] + [jnp.where(z >= k, up[k], down[n - k]) for k in range(1, n)]
    return jnp.concatenate(slots, axis=0)


def line_scatter(full, n):
    rows = full.shape[0] // n
    part = [lax.slice_in_dim(full, k * rows, (k + 1) * rows) for k in range(n)]
    up = down = None
    for s in range(1, n):
        a = part[s] if up is None else part[s] + up.astype(F32)
        b = part[n - s] if down is None else part[n - s] + down.astype(F32)
        up = lax.ppermute(a.astype(BF16), "outer", [(i, i + 1) for i in range(0, s)])
        down = lax.ppermute(b.astype(BF16), "outer", [(i, i - 1) for i in range(n - s, n)])
    return part[0] + up.astype(F32) + down.astype(F32)


def local(
    tokens, lengths, w_qkv, b_qkv, w_out, b_out, w_fc, b_fc, w_proj, b_proj,
    gain_attn, shift_attn, gain_mlp, shift_mlp, cotangent,
):
    n = lax.axis_size("outer")
    z = lax.axis_index("outer")
    inner = lax.axis_index("inner")
    tensor = lax.axis_index("tensor")
    n_tensor = lax.axis_size("tensor")
    own_rows, width = tokens.shape
    group_rows = own_rows * n_tensor
    block = width // n
    heads = w_qkv.shape[1]
    per = heads // INNER
    ff = w_fc.shape[1] // INNER
    wide = ff // CHUNKS

    def turn(v):
        parts = v.reshape(v.shape[:-1] + (n, block))
        return jnp.concatenate(
            [lax.dynamic_index_in_dim(parts, lax.rem(z - k + n, n), v.ndim - 1, False) for k in range(n)],
            axis=-1,
        )

    def spread_cols(w, pieces):
        rows = w.shape[0]
        w = w.reshape(rows, INNER, -1)
        return lax.all_to_all(w, "inner", 1, 0, tiled=False).reshape(INNER * rows, -1)

    lens = lax.all_gather(lengths, "inner", axis=0, tiled=True)
    x_turned = turn(tokens)
    own_index = tensor * own_rows + jnp.arange(own_rows, dtype=jnp.int32)
    own_live = (layout(lengths[0], own_index)[0] < 2).astype(F32)[:, None]
    cot_float = cotangent.astype(F32)
    grad_own = cot_float * own_live
    x_all = lax.all_gather(x_turned, ("inner", "tensor"), axis=0, tiled=True)
    grad_branch = lax.all_gather(turn(grad_own.astype(BF16)), ("inner", "tensor"), axis=0, tiled=True)

    fc_rows = spread_cols(w_fc, 1)
    proj_rows = spread_cols(w_proj, 1)
    qkv_rows = spread_cols(w_qkv.reshape(w_qkv.shape[0], -1), 1)
    out_rows = spread_cols(w_out.reshape(w_out.shape[0], -1), 1)

    def gather_mlp(c):
        cols = slice(c * wide, (c + 1) * wide)
        return line_gather(fc_rows[:, cols], z, n), line_gather(proj_rows[:, cols], z, n)

    ga, sa, gm, sm = turn(gain_attn), turn(shift_attn), turn(gain_mlp), turn(shift_mlp)
    xhat, _ = norm_stats(x_all.astype(F32))
    normed_attn = (xhat * ga + sa).astype(BF16)
    normed_mlp = (xhat * gm + sm).astype(BF16)
    b_fc_own = lax.dynamic_slice_in_dim(b_fc, inner * ff, ff)
    b_qkv_own = lax.dynamic_slice_in_dim(b_qkv, inner * per, per).reshape(-1)

    hidden_all, pre_all, fc_all, proj_all = [], [], [], []
    sum_fc, sum_proj, bias_fc = [], [], []

    def mlp(c):
        fc, proj = gather_mlp(c)
        hidden_pre = dot(normed_mlp, fc, NN) + b_fc_own[c * wide : (c + 1) * wide]
        hidden = jax.nn.gelu(hidden_pre, approximate=False).astype(BF16)
        sum_proj.append(line_scatter(dot(grad_branch, hidden, TN), n))
        grad_pre = (dot(grad_branch, proj, NN) * gelu_slope(hidden_pre)).astype(BF16)
        sum_fc.append(line_scatter(dot(normed_mlp, grad_pre, TN), n))
        bias_fc.append(jnp.sum(grad_pre.astype(F32), axis=0))
        hidden_all.append(hidden)
        pre_all.append(grad_pre)
        fc_all.append(fc)
        proj_all.append(proj)

    mlp(0)

    qkv = line_gather(qkv_rows, z, n)
    out = line_gather(out_rows, z, n)
    t_all = x_all.shape[0]
    groups = t_all // group_rows
    row_index = jnp.arange(group_rows, dtype=jnp.int32)
    segment, position = jax.vmap(lambda l: layout(l, row_index))(lens)
    cosine, sine_part = angles(position)
    cosine, sine_part = cosine[:, :, None], sine_part[:, :, None]
    joined = (dot(normed_attn, qkv, NN) + b_qkv_own).reshape(groups, group_rows, per, 3 * HEAD)
    queries = rotary(joined[..., :HEAD], cosine, sine_part).astype(BF16)
    key_rot = rotary(joined[..., HEAD : 2 * HEAD], cosine, sine_part).astype(BF16)
    values = joined[..., 2 * HEAD :].astype(BF16)
    scale = 1.0 / math.sqrt(HEAD)
    scores = jnp.einsum("gqhe,gkhe->ghqk", queries, key_rot, preferred_element_type=F32) * scale
    allowed = (segment[:, :, None] == segment[:, None, :]) & (row_index[:, None] >= row_index[None, :])
    scores = jnp.where(allowed[:, None], scores, -1e30)
    shifted = jnp.exp(scores - jnp.max(scores, axis=-1, keepdims=True))
    probs = shifted / jnp.sum(shifted, axis=-1, keepdims=True)
    probs_low = probs.astype(BF16)
    mixed = jnp.einsum("ghqk,gkhe->gqhe", probs_low, values, preferred_element_type=F32).astype(BF16)
    mixed_flat = mixed.reshape(t_all, per * HEAD)
    sum_out = line_scatter(dot(grad_branch, mixed_flat, TN), n)
    grad_mixed = dot(grad_branch, out, NN).astype(BF16).reshape(groups, group_rows, per, HEAD)
    grad_probs = jnp.einsum("gqhe,gkhe->ghqk", grad_mixed, values, preferred_element_type=F32)
    grad_scores = (
        probs * (grad_probs - jnp.sum(probs * grad_probs, axis=-1, keepdims=True))
    ).astype(BF16)
    grad_values = jnp.einsum("ghqk,gqhe->gkhe", probs_low, grad_mixed, preferred_element_type=F32)
    grad_queries = jnp.einsum("ghqk,gkhe->gqhe", grad_scores, key_rot, preferred_element_type=F32) * scale
    grad_keys = jnp.einsum("ghqk,gqhe->gkhe", grad_scores, queries, preferred_element_type=F32) * scale
    grad_joined = jnp.concatenate(
        [rotary(grad_queries, cosine, -sine_part), rotary(grad_keys, cosine, -sine_part), grad_values],
        axis=-1,
    ).astype(BF16).reshape(t_all, per * 3 * HEAD)
    sum_qkv = line_scatter(dot(normed_attn, grad_joined, TN), n)
    bias_qkv = jnp.sum(grad_joined.astype(F32), axis=0)

    for c in range(1, CHUNKS):
        mlp(c)

    left = jnp.concatenate(hidden_all + [mixed_flat], axis=1)
    right = jnp.concatenate(proj_all + [out], axis=1)
    branch = dot(left, right, NT).astype(BF16)
    branch_own = lax.psum_scatter(branch, ("inner", "tensor"), scatter_dimension=0, tiled=True)
    n_attn = dot(grad_joined, qkv, NT)
    n_mlp = dot(jnp.concatenate(pre_all, axis=1), jnp.concatenate(fc_all, axis=1), NT)
    u = (n_attn * ga + n_mlp * gm).astype(BF16)
    u_own = lax.psum_scatter(u, ("inner", "tensor"), scatter_dimension=0, tiled=True).astype(F32)

    def back(v):
        parts = v.reshape(v.shape[:-1] + (n, block))
        return jnp.concatenate(
            [lax.dynamic_index_in_dim(parts, lax.rem(z - k + n, n), v.ndim - 1, False) for k in range(n)],
            axis=-1,
        )

    residual = tokens.astype(F32)
    own_hat, own_inv = norm_stats(residual)
    output = residual + own_live * (back(branch_own).astype(F32) + b_out + b_proj)
    u_back = back(u_own)
    grad_tokens = cot_float + own_inv * (
        u_back
        - jnp.mean(u_back, axis=-1, keepdims=True)
        - own_hat * jnp.mean(u_back * own_hat, axis=-1, keepdims=True)
    )

    cols = jnp.stack(
        [
            jnp.sum(n_attn * xhat, axis=0),
            jnp.sum(n_attn, axis=0),
            jnp.sum(n_mlp * xhat, axis=0),
            jnp.sum(n_mlp, axis=0),
        ]
    )
    cols = jnp.concatenate([jnp.sum(grad_own, axis=0)[None], back(cols)], axis=0)
    place = tensor * INNER + inner
    full_qkv = jnp.zeros((n_tensor * INNER, per * 3 * HEAD), F32)
    full_qkv = lax.dynamic_update_index_in_dim(full_qkv, bias_qkv, place, 0)
    full_fc = jnp.zeros((n_tensor * INNER, ff), F32)
    full_fc = lax.dynamic_update_index_in_dim(full_fc, jnp.concatenate(bias_fc), place, 0)
    flat = lax.psum(
        jnp.concatenate([cols.reshape(-1), full_qkv.reshape(-1), full_fc.reshape(-1)]),
        ("outer", "inner", "tensor"),
    )
    cols = flat[: 5 * width].reshape(5, width)
    g_qkv = flat[5 * width : 5 * width + full_qkv.size].reshape(n_tensor, heads, 3 * HEAD)
    g_fc = flat[5 * width + full_qkv.size :].reshape(n_tensor, INNER * ff)

    def collect(own):
        rows = own.shape[0] // INNER
        got = lax.all_to_all(own.astype(BF16).reshape(INNER, rows, -1), "inner", 0, 1, tiled=False)
        return got.reshape(rows, -1).astype(F32)

    return (
        output.astype(BF16),
        grad_tokens.astype(BF16),
        collect(sum_qkv).reshape(w_qkv.shape),
        lax.dynamic_index_in_dim(g_qkv, tensor, 0, False),
        collect(sum_out).reshape(w_out.shape),
        cols[0],
        collect(jnp.concatenate(sum_fc, axis=1)),
        lax.dynamic_index_in_dim(g_fc, tensor, 0, False),
        collect(jnp.concatenate(sum_proj, axis=1)),
        cols[0],
        cols[1],
        cols[2],
        cols[3],
        cols[4],
    )


def solution(mesh):
    n_dp, n_tensor = mesh.devices.shape
    split = Mesh(
        mesh.devices.reshape(n_dp // INNER, INNER, n_tensor), ("outer", "inner", "tensor")
    )
    dp = ("outer", "inner")
    rows = P(("outer", "inner", "tensor"), None)
    w3 = P(dp, "tensor", None)
    w2 = P(dp, "tensor")
    return jax.shard_map(
        local,
        mesh=split,
        in_specs=(
            rows, P(dp, None), w3, P("tensor", None), w3, P(), w2, P("tensor"), w2, P(),
            P(), P(), P(), P(), rows,
        ),
        out_specs=(
            rows, rows, w3, P("tensor", None), w3, P(), w2, P("tensor"), w2, P(), P(), P(), P(), P(),
        ),
        check_vma=False,
    )
```

```python
import functools
import math

import jax
import jax.numpy as jnp
from jax import lax
from jax.experimental import pallas as pl
from jax.experimental.pallas import tpu as pltpu
from jax.sharding import Mesh
from jax.sharding import PartitionSpec as P

HEAD = 256
ROT = 64
INNER = 4
UNITS = 12
UNIT = 256
F32 = jnp.float32
BF16 = jnp.bfloat16
MESH = pl.DeviceIdType.MESH
NN = (((1,), (0,)), ((), ()))
NT = (((1,), (1,)), ((), ()))
TN = (((0,), (0,)), ((), ()))


def dot(a, b, dims=NN):
    return lax.dot_general(a, b, dims, preferred_element_type=F32)


def kernel(
    n, tokens, cot, cotm, win, pay, tcos, tsin, b_qkv, b_fc, vecs,
    out_ref, gtok_ref, sums_ref, gw_ref, xa, rbuf, fc_buf, fh_buf, fb_buf,
    W, LB, RT, HP, STG, INB, PB, FIN, XT, SVR, LENB, BQ, BF,
    p_ss, p_rs, a_ss, a_rs, a_ls, g_ss, g_rs, r_ss, r_rs, r_ls, o_ss, o_rs, o_ls,
    x_ss, x_rs, x_ls, f_ss, f_rs, h_ss, h_rs, fl, v_ss, v_rs, loc,
):
    z = lax.axis_index("outer")
    i = lax.axis_index("inner")
    y = lax.axis_index("tensor")
    rows = tokens.shape[0]
    width = tokens.shape[1]
    B = width // n
    R = B // INNER
    group = 2 * rows
    groups = INNER
    tall = groups * group
    iC = i + 1 - 2 * lax.rem(i, 2)
    iX = lax.rem(i + 2, INNER)
    iXC = INNER - 1 - i
    inner_peers = (iC, iX, iXC)
    dC, dX, dY = {"inner": iC}, {"inner": iX}, {"tensor": 1 - y}
    steps = [dC, dX, dY]
    k = 1
    while k < n:
        steps.append({"outer": z + k * (1 - 2 * lax.rem(z // k, 2))})
        k *= 2

    def ds(start, size, mult):
        return pl.ds(pl.multiple_of(start, mult), size)

    def remote(src, dst, ss, rs, dev):
        return pltpu.make_async_remote_copy(
            src_ref=src, dst_ref=dst, send_sem=ss, recv_sem=rs, device_id=dev, device_id_type=MESH
        )

    bar = pltpu.get_barrier_semaphore()
    greet = steps[:3] + [{"inner": iXC}] + steps[4:]
    for dev in greet:
        pl.semaphore_signal(bar, inc=1, device_id=dev, device_id_type=MESH)

    @pl.when(z > 0)
    def _():
        pl.semaphore_signal(bar, inc=1, device_id={"outer": z - 1}, device_id_type=MESH)

    @pl.when(z < n - 1)
    def _():
        pl.semaphore_signal(bar, inc=1, device_id={"outer": z + 1}, device_id_type=MESH)

    pl.semaphore_wait(bar, len(greet) + (z + n - 1) // n + (2 * n - 2 - z) // n)

    def a2a_copy(u, p):
        dst = W.at[u, ds(z * B + i * R, R, R)]
        return remote(win.at[inner_peers[p], u], dst, a_ss.at[u, p], a_rs.at[u, p], {"inner": inner_peers[p]})

    def a2a_own(u):
        return pltpu.make_async_copy(win.at[i, u], W.at[u, ds(z * B + i * R, R, R)], a_ls.at[u])

    def a2a(u):
        for p in range(3):
            a2a_copy(u, p).start()
        a2a_own(u).start()

    def g_copy(u, j, e, s):
        blk = W.at[u, ds(j * B, B, B)]
        return remote(blk, blk, g_ss.at[e, s], g_rs.at[u, j], {"outer": z + 1 - 2 * e})

    def start_own(u):
        for p in range(3):
            a2a_copy(u, p).wait_recv()
        a2a_own(u).wait()
        for e in range(2):
            @pl.when((z < n - 1) if e == 0 else (z > 0))
            def _():
                @pl.when(u > 0)
                def _():
                    g_copy(u, z, e, 0).wait_send()

                g_copy(u, z, e, 0).start()

    def pass_on(u, s):
        for e in range(2):
            sgn = 1 - 2 * e
            j = z - sgn * s

            @pl.when((j >= 0) & (j < n))
            def _():
                g_copy(u, j, e, s).wait_recv()

                @pl.when((z < n - 1) if e == 0 else (z > 0))
                def _():
                    @pl.when(u > 0)
                    def _():
                        g_copy(u, j, e, s).wait_send()

                    g_copy(u, j, e, s).start()

    def gather_round(t):
        @pl.when(t + 1 < UNITS)
        def _():
            start_own(t + 1)

        @pl.loop(1, n)
        def _(s):
            u = t + 1 - s

            @pl.when((u >= 0) & (u < UNITS))
            def _():
                pass_on(u, s)

    def left(v):
        high = (v + 12) // 16
        return high * lax.rem(v, 2) * 2 + (1 - high) * ((v + 2) // 3)

    def r_copy(v, e, s):
        return remote(
            STG.at[e, s], rbuf.at[v, e, s], r_ss.at[e, s], r_rs.at[v, e, s], {"outer": z + 1 - 2 * e}
        )

    def r_load(v, e, s):
        return pltpu.make_async_copy(rbuf.at[v, e, s], INB.at[e], r_ls.at[e])

    def partial(v, d):
        PB[...] = dot(RT[v], LB[left(v), :, ds(d * B, B, 128)])

    def sum_step(v, s):
        for e in range(2):
            sgn = 1 - 2 * e
            d = z + sgn * (n - s)

            @pl.when((d >= 0) & (d < n))
            def _():
                before = (z > 0) if e == 0 else (z < n - 1)

                @pl.when(before)
                def _():
                    r_copy(v, e, s - 1).wait_recv()
                    r_load(v, e, s - 1).start()

                partial(v, d)

                @pl.when(v > 0)
                def _():
                    r_copy(v, e, s).wait_send()

                @pl.when(before)
                def _():
                    r_load(v, e, s - 1).wait()
                    PB[...] += INB[e].astype(F32)

                STG[e, s] = PB[...].astype(BF16)
                r_copy(v, e, s).start()

    def o_copy(v, slot, p):
        return remote(
            FIN.at[slot, ds(inner_peers[p] * R, R, R)],
            gw_ref.at[v, :, ds(i * UNIT, UNIT, UNIT)],
            o_ss.at[slot, p],
            o_rs.at[v, p],
            {"inner": inner_peers[p]},
        )

    def o_own(v, slot):
        return pltpu.make_async_copy(
            FIN.at[slot, ds(i * R, R, R)], gw_ref.at[v, :, ds(i * UNIT, UNIT, UNIT)], o_ls.at[slot]
        )

    def finish(v):
        slot = lax.rem(v, 2)
        for e in range(2):
            @pl.when((z > 0) if e == 0 else (z < n - 1))
            def _():
                r_copy(v, e, n - 1).wait_recv()
                r_load(v, e, n - 1).start()

        partial(v, z)
        for e in range(2):
            @pl.when((z > 0) if e == 0 else (z < n - 1))
            def _():
                r_load(v, e, n - 1).wait()
                PB[...] += INB[e].astype(F32)

        @pl.when(v > 1)
        def _():
            for p in range(3):
                o_copy(v, slot, p).wait_send()
            o_own(v, slot).wait()

        FIN[slot] = PB[...].T
        for p in range(3):
            o_copy(v, slot, p).start()
        o_own(v, slot).start()

    def sum_round(t):
        @pl.loop(1, n)
        def _(s):
            v = t + 1 - s

            @pl.when((v >= 0) & (v < UNITS))
            def _():
                sum_step(v, s)

        v = t + 1 - n

        @pl.when((v >= 0) & (v < UNITS))
        def _():
            finish(v)

    def block_of(fx, fy, fc):
        at = lax.rem(i + 2 * fx, INNER)
        at = at + fc * (1 - 2 * lax.rem(at, 2))
        return at * 2 + lax.rem(y + fy, 2)

    def block_rows(k):
        return block_of(lax.rem(k, 2), lax.rem(k // 2, 2), k // 4)

    half = rows // 2

    def part(ref, b, which=None):
        if which is None:
            return ref.at[ds(b * rows, rows, rows)]
        return ref.at[ds(b * rows + which * half, half, half)]

    own_b, x_b, y_b, d_b = (block_of(a, b, 0) for a, b in ((0, 0), (1, 0), (0, 1), (1, 1)))

    def x_sends(a, src, dst):
        def mk(k, s, d, dev):
            return remote(s, d, x_ss.at[a, k], x_rs.at[a, k], dev)

        return [
            mk(0, src, part(dst, own_b), dX),
            mk(1, src, part(dst, own_b), dY),
            mk(2, src, part(dst, own_b), dC),
            mk(3, part(dst, x_b, 0), part(dst, x_b, 0), dY),
            mk(4, part(dst, y_b, 1), part(dst, y_b, 1), dX),
            mk(5, part(dst, x_b), part(dst, x_b), dC),
            mk(6, part(dst, y_b), part(dst, y_b), dC),
            mk(7, part(dst, d_b), part(dst, d_b), dC),
        ]

    gb_ref = LB.at[0]
    xs = x_sends(0, tokens, xa)
    cs = x_sends(1, cotm, gb_ref)
    x_local = pltpu.make_async_copy(tokens, part(xa, own_b), x_ls.at[0])
    c_local = pltpu.make_async_copy(cotm, part(gb_ref, own_b), x_ls.at[1])

    def spread_first(ops, local):
        for op in ops[:3]:
            op.start()
        local.start()

    def spread_second(ops):
        ops[0].wait_recv()
        ops[3].start()
        ops[5].start()
        ops[1].wait_recv()
        ops[4].start()
        ops[6].start()

    def spread_third(ops):
        ops[3].wait_recv()
        ops[4].wait_recv()
        ops[7].start()

    def load_x(b):
        cp = pltpu.make_async_copy(part(xa, b), XT, loc.at[0])
        cp.start()
        cp.wait()

    def stats(v):
        mean = jnp.mean(v, axis=-1, keepdims=True)
        center = v - mean
        inv = lax.rsqrt(jnp.mean(center * center, axis=-1, keepdims=True) + 1e-05)
        return center * inv, inv

    def norm_block(k):
        b = block_rows(k)
        load_x(b)

        @pl.loop(0, rows // 32)
        def _(t):
            at = ds(t * 32, 32, 32)
            to = ds(b * rows + t * 32, 32, 32)
            hat, _ = stats(XT[at].astype(F32))
            LB[1, to] = (hat * vecs[0:1] + vecs[1:2]).astype(BF16)
            LB[2, to] = (hat * vecs[2:3] + vecs[3:4]).astype(BF16)

    def p_copy(p):
        return remote(pay, LENB.at[i], p_ss.at[p], p_rs.at[p], {"inner": inner_peers[p]})

    for p in range(3):
        p_copy(p).start()
    p_own = pltpu.make_async_copy(pay, LENB.at[i], loc.at[1])
    p_own.start()
    a2a(0)
    spread_first(xs, x_local)
    for u in range(1, 4):
        a2a(u)
    start_own(0)
    gather_round(0)
    x_local.wait()
    norm_block(0)
    spread_second(xs)
    spread_first(cs, c_local)
    gather_round(1)
    xs[2].wait_recv()

    @pl.loop(0, 3)
    def _(k):
        norm_block(1 + k + k // 2)

    spread_third(xs)
    for u in range(4, 6):
        a2a(u)
    gather_round(2)
    spread_second(cs)
    for u in range(6, UNITS):
        a2a(u)
    for k in (5, 6, 7):
        xs[k].wait_recv()

    @pl.loop(0, 4)
    def _(k):
        norm_block(3 + k + (k + 2) // 3)

    spread_third(cs)

    @pl.loop(3, n + 1)
    def _(t):
        gather_round(t)

    for p in range(3):
        p_copy(p).wait_recv()
    p_own.wait()

    scale = 1.0 / math.sqrt(HEAD)
    lane = lax.broadcasted_iota(jnp.int32, (group, 128), 1)
    row_at = lax.broadcasted_iota(jnp.int32, (group, 1), 0).astype(F32)
    q_at = lax.broadcasted_iota(jnp.int32, (group, group), 0)
    k_at = lax.broadcasted_iota(jnp.int32, (group, group), 1)

    def turning(g):
        info = LENB[g]
        a, ab = info[4:5, 0:1], info[5:6, 0:1]
        in_a = row_at < a
        in_b = row_at < ab
        ca = jnp.where(in_a, 1.0, jnp.where(in_b, info[0:1], info[2:3]))
        sa = jnp.where(in_a, 0.0, jnp.where(in_b, info[1:2], info[3:4]))
        cosine = tcos[...] * ca + tsin[...] * sa
        sine = tsin[...] * ca - tcos[...] * sa
        low = jnp.where(lane < ROT // 2, -sine, 0.0)
        high = jnp.where(lane < ROT // 2, 0.0, sine)
        begin = jnp.where(in_a, 0.0, jnp.where(in_b, a, ab)).astype(jnp.int32)
        return cosine, low, high, begin

    def turn(v, cosine, low, high):
        first = v[:, :128]
        first = (
            first * cosine
            + pltpu.roll(first, 128 - ROT // 2, 1) * low
            + pltpu.roll(first, ROT // 2, 1) * high
        )
        return jnp.concatenate([first, v[:, 128:]], axis=1)

    def keep(slot, g, v):
        for h in range(group // 256):
            RT[slot, :, ds(g * group + h * 256, 256, 256)] = v[h * 256 : (h + 1) * 256]

    def kept(slot, g):
        return jnp.concatenate(
            [RT[slot, :, ds(g * group + h * 256, 256, 256)] for h in range(group // 256)], axis=0
        )

    def softmax(q, kk, begin):
        scores = dot(q, kk, NT) * scale
        allowed = (k_at <= q_at) & (k_at >= begin)
        scores = jnp.where(allowed, scores, -1e30)
        shifted = jnp.exp(scores - jnp.max(scores, axis=-1, keepdims=True))
        return shifted / jnp.sum(shifted, axis=-1, keepdims=True)

    @pl.loop(0, groups)
    def _(g):
        at = ds(g * group, group, group)
        cosine, low, high, begin = turning(g)
        nm = LB[1, at]
        q = turn(dot(nm, W[0]) + b_qkv[0:1], cosine, low, high).astype(BF16)
        keep(4, g, q)
        kk = turn(dot(nm, W[1]) + b_qkv[1:2], cosine, low, high).astype(BF16)
        keep(5, g, kk)
        vv = (dot(nm, W[2]) + b_qkv[2:3]).astype(BF16)
        keep(6, g, vv)
        probs = softmax(q, kk, begin).astype(BF16)
        mixed = dot(probs, vv).astype(BF16)
        RT[0, :, at] = mixed.T

    gather_round(n + 1)
    c_local.wait()
    cs[2].wait_recv()
    for k in (5, 6, 7):
        cs[k].wait_recv()
    sum_round(0)
    BQ[...] = jnp.zeros_like(BQ)
    BF[...] = jnp.zeros_like(BF)

    @pl.loop(0, groups)
    def _(g):
        at = ds(g * group, group, group)
        cosine, low, high, begin = turning(g)
        q, kk, vv = kept(4, g), kept(5, g), kept(6, g)
        probs = softmax(q, kk, begin)
        gm = dot(LB[0, at], W[3]).astype(BF16)
        gp = dot(gm, vv, NT)
        gs = (probs * (gp - jnp.sum(probs * gp, axis=-1, keepdims=True))).astype(BF16)
        gv = dot(probs.astype(BF16), gm, TN).astype(BF16)
        gq = turn(dot(gs, kk) * scale, cosine, -low, -high).astype(BF16)
        gk = turn(dot(gs, q, TN) * scale, cosine, -low, -high).astype(BF16)
        for r, val in enumerate((gq, gk, gv)):
            RT[1 + r, :, at] = val.T
            BQ[r : r + 1] += jnp.sum(val.astype(F32), axis=0, keepdims=True)

    gather_round(n + 2)
    sum_round(1)
    gather_round(n + 3)

    @pl.loop(0, (UNITS - 4) // 2)
    def _(c):
        u = 4 + 2 * c

        @pl.loop(0, groups)
        def _(g):
            at = ds(g * group, group, group)
            pre = dot(LB[2, at], W[u]) + b_fc[c]
            for h in range(group // 256):
                HP[:, ds(g * group + h * 256, 256, 256)] = pre[h * 256 : (h + 1) * 256]
            phi = 0.5 * (1.0 + lax.erf(pre * (1.0 / math.sqrt(2.0))))
            RT[u, :, at] = (pre * phi).astype(BF16).T

        sum_round(2 + 2 * c)
        gather_round(n + 4 + 2 * c)

        @pl.loop(0, groups)
        def _(g):
            at = ds(g * group, group, group)
            gh = dot(LB[0, at], W[u + 1])
            pre = jnp.concatenate(
                [HP[:, ds(g * group + h * 256, 256, 256)] for h in range(group // 256)], axis=0
            )
            slope = 0.5 * (1.0 + lax.erf(pre * (1.0 / math.sqrt(2.0)))) + pre * jnp.exp(
                -0.5 * pre * pre
            ) * (1.0 / math.sqrt(2.0 * math.pi))
            val = (gh * slope).astype(BF16)
            BF[c] += jnp.sum(val.astype(F32), axis=0, keepdims=True)
            RT[u + 1, :, at] = val.T

        sum_round(3 + 2 * c)
        gather_round(n + 5 + 2 * c)

    clear = max(10, n + 3)
    if clear > 10:
        @pl.loop(10, clear)
        def _(t):
            sum_round(t)

    tail = iter(range(clear, 10 + n + 1))
    FS = LB.at[1]
    wide = 512

    def slot(k):
        return FS.at[pl.ds(k * rows, rows)]

    sums_ref[...] = jnp.zeros_like(sums_ref)
    sums_ref[4:5] = jnp.sum(LB[0, ds(own_b * rows, rows, rows)].astype(F32), axis=0, keepdims=True)
    for r in range(3):
        sums_ref[pl.ds(5 + i, 1), r * UNIT : (r + 1) * UNIT] = BQ[r : r + 1]
    for c in range(4):
        sums_ref[pl.ds(5 + i, 1), (3 + c) * UNIT : (4 + c) * UNIT] = BF[c]

    def branch_block(b):
        at = ds(b * rows, rows, rows)
        lhs = [RT[v, :, at] for v in (0, 4, 6, 8, 10)]

        @pl.loop(0, width // wide)
        def _(t):
            to = ds(t * wide, wide, wide)
            acc = dot(lhs[0], W[3, to], (((0,), (1,)), ((), ())))
            for k, u in enumerate((5, 7, 9, 11)):
                acc += dot(lhs[1 + k], W[u, to], (((0,), (1,)), ((), ())))
            HP[:, to] = acc

    def input_block(b):
        at = ds(b * rows, rows, rows)
        load_x(b)
        v = XT[...].astype(F32)
        mean = jnp.mean(v, axis=-1, keepdims=True)
        center = v - mean
        inv = lax.rsqrt(jnp.mean(center * center, axis=-1, keepdims=True) + 1e-05)

        @pl.loop(0, width // wide)
        def _(t):
            to = ds(t * wide, wide, wide)
            na = dot(RT[1, :, at], W[0, to], (((0,), (1,)), ((), ())))
            for k in (1, 2):
                na += dot(RT[1 + k, :, at], W[k, to], (((0,), (1,)), ((), ())))
            nm = dot(RT[5, :, at], W[4, to], (((0,), (1,)), ((), ())))
            for u in (6, 8, 10):
                nm += dot(RT[u + 1, :, at], W[u, to], (((0,), (1,)), ((), ())))
            hat = (XT[:, to].astype(F32) - mean) * inv
            sums_ref[0:1, to] += jnp.sum(na * hat, axis=0, keepdims=True)
            sums_ref[1:2, to] += jnp.sum(na, axis=0, keepdims=True)
            sums_ref[2:3, to] += jnp.sum(nm * hat, axis=0, keepdims=True)
            sums_ref[3:4, to] += jnp.sum(nm, axis=0, keepdims=True)
            HP[:, to] = na * vecs[0:1, to] + nm * vecs[2:3, to]

    def c_copy(a, k):
        return remote(slot(k % 2), fc_buf.at[a, k], f_ss.at[k % 2], f_rs.at[a, k], dC)

    def h_copies(a):
        return (
            remote(FS.at[pl.ds(2 * rows, half)], fh_buf.at[a, 0], h_ss.at[0], h_rs.at[a, 0], dX),
            remote(FS.at[pl.ds(2 * rows + half, half)], fh_buf.at[a, 1], h_ss.at[1], h_rs.at[a, 1], dY),
            remote(slot(3), fb_buf.at[a, 0], h_ss.at[2], h_rs.at[a, 2], dX),
            remote(slot(4), fb_buf.at[a, 1], h_ss.at[3], h_rs.at[a, 3], dY),
        )

    def fold(a, block):
        hs = h_copies(a)
        for k in range(4):
            block(block_of((3 - k) // 2, (3 - k) % 2, 1))
            if k >= 2 or a > 0:
                c_copy(a, k).wait_send()
            slot(k % 2)[...] = HP[...].astype(BF16)
            c_copy(a, k).start()
        t = next(tail, None)
        if t is not None:
            sum_round(t)
        for k in range(4):
            c_copy(a, k).wait_recv()
            get = pltpu.make_async_copy(fc_buf.at[a, k], slot(5), fl.at[0])
            get.start()
            extra = []
            if k == 1:
                hs[1].wait_recv()
                extra.append((pltpu.make_async_copy(fh_buf.at[a, 1], FS.at[pl.ds(6 * rows, half)], fl.at[1]), half))
            if k == 2:
                hs[0].wait_recv()
                extra.append((pltpu.make_async_copy(fh_buf.at[a, 0], FS.at[pl.ds(6 * rows, half)], fl.at[1]), 0))
            for cp, _ in extra:
                cp.start()
            block(block_of((3 - k) // 2, (3 - k) % 2, 0))
            get.wait()
            HP[...] += slot(5)[...].astype(F32)
            for cp, at in extra:
                cp.wait()
                HP[at : at + half] += FS[pl.ds(6 * rows, half)].astype(F32)
            if k < 3:
                if a > 0:
                    for op in (hs[0], hs[1]) if k == 0 else (hs[k + 1],):
                        op.wait_send()
                slot(2 + k)[...] = HP[...].astype(BF16)
                for op in (hs[0], hs[1]) if k == 0 else (hs[k + 1],):
                    op.start()
            if k in (0, 2):
                t = next(tail, None)
                if t is not None:
                    sum_round(t)
        for j in range(2):
            hs[2 + j].wait_recv()
            get = pltpu.make_async_copy(fb_buf.at[a, j], slot(6), fl.at[1])
            get.start()
            get.wait()
            HP[...] += slot(6)[...].astype(F32)

    fold(0, branch_block)
    own_first = y * rows
    info = LENB[i]

    load_x(own_b)

    @pl.loop(0, rows // 32)
    def _(t):
        at = ds(t * 32, 32, 32)
        pos = (own_first + t * 32 + lax.broadcasted_iota(jnp.int32, (32, 1), 0)).astype(F32)
        live = (pos < info[5:6, 0:1]).astype(F32)
        res = XT[at].astype(F32) + live * (HP[at] + vecs[4:5])
        FS[ds(7 * rows + t * 32, 32, 32)] = res.astype(BF16)

    put = pltpu.make_async_copy(slot(7), out_ref, fl.at[2])
    put.start()
    fold(1, input_block)
    put.wait()

    def v_copy(k):
        return remote(sums_ref, SVR.at[k], v_ss.at[k], v_rs.at[k], steps[k])

    keep_row = lax.broadcasted_iota(jnp.int32, (16, 1), 0) < 5
    v_copy(0).start()

    load_x(own_b)
    get = pltpu.make_async_copy(cot, slot(6), fl.at[1])
    get.start()
    get.wait()

    @pl.loop(0, rows // 32)
    def _(t):
        at = ds(t * 32, 32, 32)
        hat, inv = stats(XT[at].astype(F32))
        u = HP[at]
        res = FS[ds(6 * rows + t * 32, 32, 32)].astype(F32) + inv * (
            u - jnp.mean(u, axis=-1, keepdims=True) - hat * jnp.mean(u * hat, axis=-1, keepdims=True)
        )
        FS[ds(7 * rows + t * 32, 32, 32)] = res.astype(BF16)

    put = pltpu.make_async_copy(slot(7), gtok_ref, fl.at[2])
    put.start()

    for k in range(len(steps)):
        if k > 0:
            v_copy(k).start()
        v_copy(k).wait()
        got = SVR[k]
        sums_ref[...] += jnp.where(keep_row, got, 0.0) if k == 2 else got

    first_left = next(tail, None)
    if first_left is not None:
        @pl.loop(first_left, 10 + n + 1)
        def _(t):
            sum_round(t)

    put.wait()

    for p in range(3):
        p_copy(p).wait_send()

    @pl.loop(0, UNITS)
    def _(u):
        for p in range(3):
            a2a_copy(u, p).wait_send()
            o_copy(u, 0, p).wait_recv()

    for op in xs + cs:
        op.wait_send()
    last = UNITS - 1
    for e in range(2):
        sgn = 1 - 2 * e
        ahead = (z < n - 1) if e == 0 else (z > 0)

        @pl.when(ahead)
        def _():
            g_copy(last, z, e, 0).wait_send()

        @pl.loop(1, n)
        def _(s):
            j = z - sgn * s
            d = z + sgn * (n - s)

            @pl.when((j >= 0) & (j < n) & ahead)
            def _():
                g_copy(last, j, e, s).wait_send()

            @pl.when((d >= 0) & (d < n))
            def _():
                r_copy(last, e, s).wait_send()

    for s in range(2):
        for p in range(3):
            o_copy(last, s, p).wait_send()
        o_own(last, s).wait()
    for k in range(2):
        c_copy(1, k).wait_send()
    for op in h_copies(1):
        op.wait_send()


def local(
    tokens, lengths, w_qkv, b_qkv, w_out, b_out, w_fc, b_fc, w_proj, b_proj,
    gain_attn, shift_attn, gain_mlp, shift_mlp, cotangent,
):
    n = lax.axis_size("outer")
    i = lax.axis_index("inner")
    y = lax.axis_index("tensor")
    rows, width = tokens.shape
    R = w_qkv.shape[0]
    B = INNER * R
    ff = w_fc.shape[1] // INNER
    group = rows * lax.axis_size("tensor")

    qkv = w_qkv.reshape(R, INNER, 3, UNIT).transpose(1, 2, 0, 3)
    out = w_out.reshape(R, INNER, 1, UNIT).transpose(1, 2, 0, 3)
    fc = w_fc.reshape(R, INNER, 4, UNIT).transpose(1, 2, 0, 3)
    proj = w_proj.reshape(R, INNER, 4, UNIT).transpose(1, 2, 0, 3)
    ffn = jnp.stack([fc, proj], axis=2).reshape(INNER, 8, R, UNIT)
    win = jnp.concatenate([qkv, out, ffn], axis=1)

    lane = jnp.arange(128)
    freq = jnp.where(
        lane < ROT, jnp.exp((lane % (ROT // 2)).astype(F32) * (2.0 / ROT) * -math.log(10000.0)), 0.0
    )
    angle = jnp.arange(group, dtype=F32)[:, None] * freq
    first = lengths[0, 0].astype(F32)
    both = first + lengths[0, 1].astype(F32)
    flat = jnp.ones((128,), F32)
    pay = jnp.stack(
        [
            jnp.cos(first * freq), jnp.sin(first * freq), jnp.cos(both * freq), jnp.sin(both * freq),
            first * flat, both * flat, 0 * flat, 0 * flat,
        ]
    )
    own_index = y * rows + jnp.arange(rows)
    live = own_index < lengths[0, 0] + lengths[0, 1]
    cotm = jnp.where(live[:, None], cotangent, jnp.zeros((), BF16))
    b_q = lax.dynamic_slice_in_dim(b_qkv, i, 1).reshape(3, HEAD)
    b_f = lax.dynamic_slice_in_dim(b_fc, i * ff, ff).reshape(4, 1, UNIT)
    zero = jnp.zeros_like(b_out)
    vecs = jnp.stack([gain_attn, shift_attn, gain_mlp, shift_mlp, b_out + b_proj, zero, zero, zero])

    tall = INNER * group
    n_steps = 3 + max(1, (n - 1).bit_length())
    hbm = pl.BlockSpec(memory_space=pl.ANY)
    vmem = pl.BlockSpec(memory_space=pltpu.VMEM)
    sds = jax.ShapeDtypeStruct
    dma = pltpu.SemaphoreType.DMA
    res = pl.pallas_call(
        functools.partial(kernel, n),
        out_shape=(
            sds((rows, width), BF16),
            sds((rows, width), BF16),
            sds((16, width), F32),
            sds((UNITS, R, INNER * UNIT), F32),
            sds((tall, width), BF16),
            sds((UNITS, 2, n, UNIT, B), BF16),
            sds((2, 4, rows, width), BF16),
            sds((2, 2, rows // 2, width), BF16),
            sds((2, 2, rows, width), BF16),
        ),
        in_specs=[hbm] * 4 + [vmem] * 6,
        out_specs=(hbm, hbm, vmem) + (hbm,) * 6,
        scratch_shapes=[
            pltpu.VMEM((UNITS, width, UNIT), BF16),
            pltpu.VMEM((3, tall, width), BF16),
            pltpu.VMEM((UNITS, UNIT, tall), BF16),
            pltpu.VMEM((UNIT, tall), F32),
            pltpu.VMEM((2, n, UNIT, B), BF16),
            pltpu.VMEM((2, UNIT, B), BF16),
            pltpu.VMEM((UNIT, B), F32),
            pltpu.VMEM((2, B, UNIT), F32),
            pltpu.VMEM((rows, width), BF16),
            pltpu.VMEM((n_steps, 16, width), F32),
            pltpu.VMEM((INNER, 8, 128), F32),
            pltpu.VMEM((8, UNIT), F32),
            pltpu.VMEM((4, 1, UNIT), F32),
            dma((3,)), dma((3,)),
            dma((UNITS, 3)), dma((UNITS, 3)), dma((UNITS,)),
            dma((2, n)), dma((UNITS, n)),
            dma((2, n)), dma((UNITS, 2, n)), dma((2,)),
            dma((2, 3)), dma((UNITS, 3)), dma((2,)),
            dma((2, 8)), dma((2, 8)), dma((2,)),
            dma((2,)), dma((2, 4)),
            dma((4,)), dma((2, 4)), dma((3,)),
            dma((n_steps,)), dma((n_steps,)), dma((2,)),
        ],
        compiler_params=pltpu.CompilerParams(
            collective_id=0, has_side_effects=True, vmem_limit_bytes=64 * 1024 * 1024 - 65536
        ),
        name="block",
    )(tokens, cotangent, cotm, win, pay, jnp.cos(angle), jnp.sin(angle), b_q, b_f, vecs)
    output, grad_tokens, sums, gw = res[:4]

    def place(units, k):
        return units.reshape(k, R, INNER, UNIT).transpose(1, 2, 0, 3).reshape(R, INNER, k * UNIT)

    g_out = place(gw[0:1], 1)
    g_qkv = place(gw[1:4], 3)
    ffn = gw[4:].reshape(4, 2, R, INNER * UNIT)
    g_proj = place(ffn[:, 0], 4).reshape(R, INNER * ff)
    g_fc = place(ffn[:, 1], 4).reshape(R, INNER * ff)
    own = sums[5 : 5 + INNER]
    return (
        output,
        grad_tokens,
        g_qkv.reshape(w_qkv.shape),
        own[:, : 3 * UNIT].reshape(b_qkv.shape),
        g_out.reshape(w_out.shape),
        sums[4],
        g_fc,
        own[:, 3 * UNIT : 3 * UNIT + ff].reshape(b_fc.shape),
        g_proj,
        sums[4],
        sums[0],
        sums[1],
        sums[2],
        sums[3],
    )


def solution(mesh):
    n_dp, n_tensor = mesh.devices.shape
    split = Mesh(
        mesh.devices.reshape(n_dp // INNER, INNER, n_tensor), ("outer", "inner", "tensor")
    )
    dp = ("outer", "inner")
    rows = P(("outer", "inner", "tensor"), None)
    w3 = P(dp, "tensor", None)
    w2 = P(dp, "tensor")
    return jax.shard_map(
        local,
        mesh=split,
        in_specs=(
            rows, P(dp, None), w3, P("tensor", None), w3, P(), w2, P("tensor"), w2, P(),
            P(), P(), P(), P(), rows,
        ),
        out_specs=(
            rows, rows, w3, P("tensor", None), w3, P(), w2, P("tensor"), w2, P(), P(), P(), P(), P(),
        ),
        check_vma=False,
    )
```

```python
import functools
import math

import jax
import jax.numpy as jnp
import numpy as np
from jax import lax
from jax.experimental import pallas as pl
from jax.experimental.pallas import tpu as pltpu
from jax.sharding import Mesh
from jax.sharding import PartitionSpec as P

HEAD = 256
ROT = 64
INNER = 4
UNITS = 12
UNIT = 256
DEPTH = 2
LAG = 2
F32 = jnp.float32
BF16 = jnp.bfloat16
MESH = pl.DeviceIdType.MESH
NN = (((1,), (0,)), ((), ()))
NT = (((1,), (1,)), ((), ()))
TN = (((0,), (0,)), ((), ()))


def dot(a, b, dims=NN):
    return lax.dot_general(a, b, dims, preferred_element_type=F32)


def kernel(
    n, tokens, cot, lens, wq, wo, w_fc, w_proj, tab, b_qkv, b_fc, b_out, b_proj,
    gain_attn, shift_attn, gain_mlp, shift_mlp,
    out_ref, gtok_ref, gq_ref, go_ref, gfc_ref, gpj_ref,
    s_gain_a, s_shift_a, s_gain_m, s_shift_m, s_bias, s_bqkv, s_bfc,
    xa, rbuf, fc_buf, fh_buf, fb_buf,
    W, LB, RT, HP, HB, STG, INB, FIN, XT, TAB, PAY, SV, SVR, LENB, BQ, BF,
    p_ss, p_rs, a_ss, a_rs, a_ls, g_ss, g_rs, r_ss, r_rs, r_ls, o_ss, o_rs, o_ls,
    x_ss, x_rs, x_ls, l_ls, f_ss, f_rs, h_ss, h_rs, fl, v_ss, v_rs, loc,
):
    z = lax.axis_index("outer")
    i = lax.axis_index("inner")
    y = lax.axis_index("tensor")
    rows, width = tokens.shape
    B = width // n
    R = B // INNER
    group = 2 * rows
    groups = INNER
    ff = UNIT * 4
    ends = z // (n - 1) + (n - 1 - z) // (n - 1)
    mid = (z > 0) & (z < n - 1)
    iC = i + 1 - 2 * lax.rem(i, 2)
    iX = lax.rem(i + 2, INNER)
    iXC = INNER - 1 - i
    inner_peers = (iC, iX, iXC)
    dC, dX, dY = {"inner": iC}, {"inner": iX}, {"tensor": 1 - y}
    steps = [dC, dX, dY]
    k = 1
    while k < n:
        steps.append({"outer": z + k * (1 - 2 * lax.rem(z // k, 2))})
        k *= 2

    def ds(start, size, mult):
        return pl.ds(pl.multiple_of(start, mult), size)

    def remote(src, dst, ss, rs, dev):
        return pltpu.make_async_remote_copy(
            src_ref=src, dst_ref=dst, send_sem=ss, recv_sem=rs, device_id=dev, device_id_type=MESH
        )

    bar = pltpu.get_barrier_semaphore()
    greet = steps[:3] + [{"inner": iXC}] + steps[4:]
    for dev in greet:
        pl.semaphore_signal(bar, inc=1, device_id=dev, device_id_type=MESH)

    @pl.when(z > 0)
    def _():
        pl.semaphore_signal(bar, inc=1, device_id={"outer": z - 1}, device_id_type=MESH)

    @pl.when(z < n - 1)
    def _():
        pl.semaphore_signal(bar, inc=1, device_id={"outer": z + 1}, device_id_type=MESH)

    pl.semaphore_wait(bar, len(greet) + (z + n - 1) // n + (2 * n - 2 - z) // n)

    def piece(u, to):
        if u < 3:
            return wq.at[to, :, pl.ds(u * UNIT, UNIT)]
        if u == 3:
            return wo.at[to]
        ref = (w_fc, w_proj)[u % 2]
        return ref.at[:, ds(to * ff + (u - 4) // 2 * UNIT, UNIT, UNIT)]

    def a2a_copy(u, p):
        dst = W.at[u, ds(z * B + i * R, R, R)]
        return remote(
            piece(u, inner_peers[p]), dst, a_ss.at[u, p], a_rs.at[u, p], {"inner": inner_peers[p]}
        )

    def a2a_own(u):
        return pltpu.make_async_copy(piece(u, i), W.at[u, ds(z * B + i * R, R, R)], a_ls.at[u])

    def a2a(*units):
        for u in units:
            for p in (1, 2, 0):
                a2a_copy(u, p).start()
            a2a_own(u).start()

    def g_copy(u, j, e, s):
        blk = W.at[u, ds(j * B, B, B)]
        return remote(blk, blk, g_ss.at[u, e, s], g_rs.at[u, j], {"outer": z + 1 - 2 * e})

    def send_own(u):
        for e in range(2):
            @pl.when((z < n - 1) if e == 0 else (z > 0))
            def _():
                g_copy(u, z, e, 0).start()

    def arrive(*units):
        for u in units:
            for p in range(3):
                a2a_copy(u, p).wait_recv()
            a2a_own(u).wait()

            @pl.when(ends > 0)
            def _():
                send_own(u)

    def own_batch(*units):
        @pl.when(mid)
        def _():
            for u in units:
                send_own(u)

    def pass_on(u, s):
        for e in range(2):
            sgn = 1 - 2 * e
            j = z - sgn * s

            @pl.when((j >= 0) & (j < n))
            def _():
                g_copy(u, j, e, s).wait_recv()

                @pl.when((z < n - 1) if e == 0 else (z > 0))
                def _():
                    g_copy(u, j, e, s).start()

    def pass_batch(first, lo, hi):
        @pl.when(mid)
        def _():
            @pl.loop(lo, hi)
            def _(s):
                @pl.loop(first, first + 3)
                def _(u):
                    pass_on(u, s)

    def need(u):
        @pl.when(ends > 0)
        def _():
            @pl.loop(1, n)
            def _(s):
                pass_on(u, s)

    def left(v):
        high = (v + 12) // 16
        return high * lax.rem(v, 2) * 2 + (1 - high) * ((v + 2) // 3)

    def stage(e, s):
        return s - 1 if e == 0 else n - 1 - s

    def r_copy(v, e, s):
        at, k = lax.rem(v, DEPTH), stage(e, s)
        return remote(
            STG.at[at, k], rbuf.at[v, e, s - 1], r_ss.at[at, k], r_rs.at[v, e, s - 1],
            {"outer": z + 1 - 2 * e},
        )

    def r_load(v, e, s):
        return pltpu.make_async_copy(rbuf.at[v, e, s - 1], INB.at[e, s - 1], r_ls.at[e, s - 1])

    def partial(v, d):
        return dot(RT[v], LB[left(v), :, ds(d * B, B, 128)])

    def before(e):
        return (z > 0) if e == 0 else (z < n - 1)

    def fetch(v, s):
        for e in range(2):
            d = z + (1 - 2 * e) * (n - s)

            @pl.when((d >= 0) & (d < n) & before(e))
            def _():
                r_copy(v, e, s - 1).wait_recv()
                r_load(v, e, s - 1).start()

    def send_sum(v, e, s, val):
        @pl.when(v >= DEPTH)
        def _():
            r_copy(v, e, s).wait_send()

        STG[lax.rem(v, DEPTH), stage(e, s)] = val.astype(BF16)
        r_copy(v, e, s).start()

    def first_step(v):
        for e in range(2):
            d = z + (1 - 2 * e) * (n - 1)

            @pl.when((d >= 0) & (d < n))
            def _():
                send_sum(v, e, 1, partial(v, d))

    def sum_step(v, s):
        for e in range(2):
            d = z + (1 - 2 * e) * (n - s)

            @pl.when((d >= 0) & (d < n))
            def _():
                @pl.when(before(e))
                def _():
                    r_load(v, e, s - 1).wait()

                send_sum(v, e, s, partial(v, d) + INB[e, s - 2].astype(F32))

    def o_copy(v, slot, p, dst):
        if p == 3:
            return pltpu.make_async_copy(FIN.at[slot, ds(i * R, R, R)], dst, o_ls.at[slot])
        src = FIN.at[slot, ds(inner_peers[p] * R, R, R)]
        return remote(src, dst, o_ss.at[slot, p], o_rs.at[v, p], {"inner": inner_peers[p]})

    def o_sent(slot):
        for p in range(3):
            o_copy(0, slot, p, go_ref.at[i]).wait_send()
        o_copy(0, slot, 3, go_ref.at[i]).wait()

    def finish(v):
        slot = lax.rem(v, 2)
        for e in range(2):
            @pl.when(before(e))
            def _():
                r_load(v, e, n - 1).wait()

        total = partial(v, z) + INB[0, n - 2].astype(F32) + INB[1, n - 2].astype(F32)

        @pl.when(v > 1)
        def _():
            o_sent(slot)

        FIN[slot] = total.T

        def go(dst):
            for p in (1, 2, 0, 3):
                o_copy(v, slot, p, dst).start()

        at = ds(i * ff + (v - 4) // 2 * UNIT, UNIT, UNIT)

        @pl.when(v == 0)
        def _():
            go(go_ref.at[i])

        @pl.when((v > 0) & (v < 4))
        def _():
            go(gq_ref.at[i, :, ds((v - 1) * UNIT, UNIT, UNIT)])

        @pl.when((v >= 4) & (lax.rem(v, 2) == 0))
        def _():
            go(gpj_ref.at[:, at])

        @pl.when((v >= 4) & (lax.rem(v, 2) == 1))
        def _():
            go(gfc_ref.at[:, at])

    def sum_round(t):
        @pl.when((t >= 0) & (t < UNITS))
        def _():
            first_step(t)

        w = t + 1 - n - LAG * ends

        @pl.loop(2, n)
        def _(s):
            v = t + 1 - s

            @pl.when((v >= 0) & (v < UNITS))
            def _():
                fetch(v, s)

        @pl.when((w >= 0) & (w < UNITS))
        def _():
            fetch(w, n)

        @pl.loop(2, n)
        def _(s):
            v = t + 1 - s

            @pl.when((v >= 0) & (v < UNITS))
            def _():
                sum_step(v, s)

        @pl.when((w >= 0) & (w < UNITS))
        def _():
            finish(w)

    def block_of(fx, fy, fc):
        at = lax.rem(i + 2 * fx, INNER)
        at = at + fc * (1 - 2 * lax.rem(at, 2))
        return at * 2 + lax.rem(y + fy, 2)

    def block_rows(k):
        return block_of(lax.rem(k, 2), lax.rem(k // 2, 2), k // 4)

    half = rows // 2

    def part(ref, b, which=None):
        if which is None:
            return ref.at[ds(b * rows, rows, rows)]
        return ref.at[ds(b * rows + which * half, half, half)]

    own_b, x_b, y_b, d_b = (block_of(a, b, 0) for a, b in ((0, 0), (1, 0), (0, 1), (1, 1)))

    def x_sends(a, src, dst):
        def mk(k, s, d, dev):
            return remote(s, d, x_ss.at[a, k], x_rs.at[a, k], dev)

        return [
            mk(0, src, part(dst, own_b), dX),
            mk(1, src, part(dst, own_b), dY),
            mk(2, src, part(dst, own_b), dC),
            mk(3, part(dst, x_b, 0), part(dst, x_b, 0), dY),
            mk(4, part(dst, y_b, 1), part(dst, y_b, 1), dX),
            mk(5, part(dst, x_b), part(dst, x_b), dC),
            mk(6, part(dst, y_b), part(dst, y_b), dC),
            mk(7, part(dst, d_b), part(dst, d_b), dC),
        ]

    gb_ref = LB.at[0]
    xs = x_sends(0, tokens, xa)
    cs = x_sends(1, part(gb_ref, own_b), gb_ref)
    x_local = pltpu.make_async_copy(tokens, part(xa, own_b), x_ls.at[0])
    c_local = pltpu.make_async_copy(cot, part(gb_ref, own_b), x_ls.at[1])

    def near(k, src=None):
        b = block_rows(k)
        return pltpu.make_async_copy(
            part(xa, b) if src is None else src, part(LB.at[2], b), l_ls.at[k]
        )

    def spread_first(ops):
        for k in (1, 0, 2):
            ops[k].start()

    def spread_second(ops):
        ops[1].wait_recv()
        ops[4].start()
        ops[6].start()
        ops[0].wait_recv()
        ops[3].start()
        ops[5].start()

    def spread_third(ops):
        ops[3].wait_recv()
        ops[4].wait_recv()
        ops[7].start()

    def stats(v):
        center = v - jnp.mean(v, axis=-1, keepdims=True)
        inv = lax.rsqrt(jnp.mean(center * center, axis=-1, keepdims=True) + 1e-05)
        return center * inv, inv

    def norm_block(k):
        b = block_rows(k)
        near(k).wait()

        @pl.loop(0, rows // 16)
        def _(t):
            to = ds(b * rows + t * 16, 16, 16)
            hat, _ = stats(LB[2, to].astype(F32))
            LB[1, to] = (hat * gain_attn[...] + shift_attn[...]).astype(BF16)
            LB[2, to] = (hat * gain_mlp[...] + shift_mlp[...]).astype(BF16)

    def p_copy(p):
        return remote(PAY, LENB.at[i], p_ss.at[p], p_rs.at[p], {"inner": inner_peers[p]})

    tab_in = pltpu.make_async_copy(tab, TAB, loc.at[0])
    tab_in.start()
    a2a(0, 1, 2)
    spread_first(xs)
    x_local.start()
    near(0, tokens).start()
    c_local.start()
    a2a(3, 4, 5)
    INB[...] = jnp.zeros_like(INB)
    BQ[...] = jnp.zeros_like(BQ)
    BF[...] = jnp.zeros_like(BF)
    tab_in.wait()
    first = lens[0, 0]
    both = first + lens[0, 1]
    for k, at in enumerate((first, both)):
        for h in range(2):
            PAY[2 * k + h : 2 * k + h + 1] = TAB[h, pl.ds(at, 1)]
        PAY[4 + k : 5 + k] = jnp.full((1, 128), at.astype(F32))
    PAY[6:8] = jnp.zeros((2, 128), F32)
    for p in range(3):
        p_copy(p).start()
    p_own = pltpu.make_async_copy(PAY, LENB.at[i], loc.at[1])
    p_own.start()
    arrive(0)
    own_batch(0)
    arrive(1, 2)
    own_batch(1, 2)
    c_local.wait()
    own_at = y * rows + lax.broadcasted_iota(jnp.int32, (16, 1), 0)

    @pl.loop(0, rows // 16)
    def _(t):
        to = ds(own_b * rows + t * 16, 16, 16)
        live = own_at + t * 16 < both
        LB[0, to] = jnp.where(live, LB[0, to].astype(F32), 0.0).astype(BF16)

    pass_batch(0, 1, 2)
    norm_block(0)
    spread_second(xs)
    spread_first(cs)
    near(1).start()
    near(2).start()
    norm_block(2)
    norm_block(1)
    pass_batch(0, 2, n - 1)
    arrive(3, 4, 5)
    own_batch(3, 4, 5)
    spread_third(xs)
    near(3).start()
    xs[2].wait_recv()
    near(4).start()
    norm_block(3)
    norm_block(4)
    x_local.wait()
    pass_batch(3, 1, 2)
    for k in (5, 6, 7):
        xs[k].wait_recv()
        near(k).start()

    @pl.loop(5, 8)
    def _(k):
        norm_block(k)

    a2a(6, 7, 8)
    for p in range(3):
        p_copy(p).wait_recv()
    p_own.wait()
    for u in range(3):
        need(u)

    scale = 1.0 / math.sqrt(HEAD)
    lane = lax.broadcasted_iota(jnp.int32, (group, 128), 1)
    row_at = lax.broadcasted_iota(jnp.int32, (group, 1), 0).astype(F32)
    q_at = lax.broadcasted_iota(jnp.int32, (group, group), 0)
    k_at = lax.broadcasted_iota(jnp.int32, (group, group), 1)

    def turning(g):
        info = LENB[g]
        a, ab = info[4:5, 0:1], info[5:6, 0:1]
        in_a = row_at < a
        in_b = row_at < ab
        ca = jnp.where(in_a, 1.0, jnp.where(in_b, info[0:1], info[2:3]))
        sa = jnp.where(in_a, 0.0, jnp.where(in_b, info[1:2], info[3:4]))
        tcos, tsin = TAB[0, :group], TAB[1, :group]
        cosine = tcos * ca + tsin * sa
        sine = tsin * ca - tcos * sa
        low = jnp.where(lane < ROT // 2, -sine, 0.0)
        high = jnp.where(lane < ROT // 2, 0.0, sine)
        begin = jnp.where(in_a, 0.0, jnp.where(in_b, a, ab)).astype(jnp.int32)
        return cosine, low, high, begin

    def turn(v, cosine, low, high):
        first = v[:, :128]
        first = (
            first * cosine
            + pltpu.roll(first, 128 - ROT // 2, 1) * low
            + pltpu.roll(first, ROT // 2, 1) * high
        )
        return jnp.concatenate([first, v[:, 128:]], axis=1)

    def keep(slot, g, v):
        for h in range(group // 256):
            RT[slot, :, ds(g * group + h * 256, 256, 256)] = v[h * 256 : (h + 1) * 256]

    def kept(slot, g):
        return jnp.concatenate(
            [RT[slot, :, ds(g * group + h * 256, 256, 256)] for h in range(group // 256)], axis=0
        )

    def softmax(q, kk, begin):
        scores = dot(q, kk, NT) * scale
        allowed = (k_at <= q_at) & (k_at >= begin)
        scores = jnp.where(allowed, scores, -1e30)
        shifted = jnp.exp(scores - jnp.max(scores, axis=-1, keepdims=True))
        return shifted / jnp.sum(shifted, axis=-1, keepdims=True)

    def attend(lo, hi):
        @pl.loop(lo, hi)
        def _(g):
            at = ds(g * group, group, group)
            cosine, low, high, begin = turning(g)
            nm = LB[1, at]
            bias = [b_qkv[pl.ds(i, 1), r * UNIT : (r + 1) * UNIT] for r in range(3)]
            q = turn(dot(nm, W[0]) + bias[0], cosine, low, high).astype(BF16)
            keep(4, g, q)
            kk = turn(dot(nm, W[1]) + bias[1], cosine, low, high).astype(BF16)
            keep(5, g, kk)
            vv = (dot(nm, W[2]) + bias[2]).astype(BF16)
            keep(6, g, vv)
            probs = softmax(q, kk, begin).astype(BF16)
            mixed = dot(probs, vv).astype(BF16)
            RT[0, :, at] = mixed.T

    attend(0, groups // 2)
    spread_second(cs)
    a2a(9, 10, 11)
    pass_batch(3, 2, n - 1)
    arrive(6, 7, 8)
    own_batch(6, 7, 8)
    attend(groups // 2, groups)
    spread_third(cs)
    cs[2].wait_recv()
    for k in (5, 6, 7):
        cs[k].wait_recv()
    sum_round(0)
    pass_batch(6, 1, 2)
    need(3)

    @pl.loop(0, groups)
    def _(g):
        at = ds(g * group, group, group)
        cosine, low, high, begin = turning(g)
        q, kk, vv = kept(4, g), kept(5, g), kept(6, g)
        probs = softmax(q, kk, begin)
        gm = dot(LB[0, at], W[3]).astype(BF16)
        gp = dot(gm, vv, NT)
        gs = (probs * (gp - jnp.sum(probs * gp, axis=-1, keepdims=True))).astype(BF16)
        gv = dot(probs.astype(BF16), gm, TN).astype(BF16)
        gq = turn(dot(gs, kk) * scale, cosine, -low, -high).astype(BF16)
        gk = turn(dot(gs, q, TN) * scale, cosine, -low, -high).astype(BF16)
        for r, val in enumerate((gq, gk, gv)):
            RT[1 + r, :, at] = val.T
            BQ[r : r + 1] += jnp.sum(val.astype(F32), axis=0, keepdims=True)

    arrive(9, 10, 11)
    sum_round(1)
    pass_batch(6, 2, n - 1)
    own_batch(9, 10, 11)

    def hidden_of(c):
        u = 4 + 2 * c
        need(u)

        @pl.loop(0, groups)
        def _(g):
            at = ds(g * group, group, group)
            pre = dot(LB[2, at], W[u]) + b_fc[:, ds(i * ff + c * UNIT, UNIT, UNIT)]
            phi = 0.5 * (1.0 + lax.erf(pre * (1.0 / math.sqrt(2.0))))
            slope = phi + pre * jnp.exp(-0.5 * pre * pre) * (1.0 / math.sqrt(2.0 * math.pi))
            for h in range(group // 256):
                HP[:, ds(g * group + h * 256, 256, 256)] = slope[h * 256 : (h + 1) * 256]
            RT[u, :, at] = (pre * phi).astype(BF16).T

    def grad_of(c):
        u = 4 + 2 * c

        @pl.loop(0, groups)
        def _(g):
            at = ds(g * group, group, group)
            gh = dot(LB[0, at], W[u + 1])
            slope = jnp.concatenate(
                [HP[:, ds(g * group + h * 256, 256, 256)] for h in range(group // 256)], axis=0
            )
            val = (gh * slope).astype(BF16)
            BF[c] += jnp.sum(val.astype(F32), axis=0, keepdims=True)
            RT[u + 1, :, at] = val.T

    FS = LB.at[1]
    wide = 512
    tiles = width // wide

    def slot(k):
        return FS.at[pl.ds(k * rows, rows)]

    LT = FS.at[pl.ds(7 * rows, rows)]

    def side(us, to):
        return jnp.concatenate([W[u, to] for u in us], axis=1)

    def turn_left(b, vs):
        at = ds(b * rows, rows, rows)
        for k, v in enumerate(vs):
            LT[:, k * UNIT : (k + 1) * UNIT] = RT[v, :, at].T

    def branch_block(b):
        turn_left(b, (0, 4, 6, 8, 10))

        @pl.loop(0, tiles)
        def _(t):
            to = ds(t * wide, wide, wide)
            HB[:, to] = dot(LT[:, : 5 * UNIT], side((3, 5, 7, 9, 11), to), NT)

    def x_block(b):
        return pltpu.make_async_copy(part(xa, b), XT, loc.at[0])

    def input_block(b):
        x_block(b).start()
        turn_left(b, (1, 2, 3, 5, 7, 9, 11))
        x_block(b).wait()
        v = XT[...].astype(F32)
        mean = jnp.mean(v, axis=-1, keepdims=True)
        center = v - mean
        inv = lax.rsqrt(jnp.mean(center * center, axis=-1, keepdims=True) + 1e-05)

        @pl.loop(0, tiles)
        def _(t):
            to = ds(t * wide, wide, wide)
            na = dot(LT[:, : 3 * UNIT], side((0, 1, 2), to), NT)
            nm = dot(LT[:, 3 * UNIT : 7 * UNIT], side((4, 6, 8, 10), to), NT)
            hat = (XT[:, to].astype(F32) - mean) * inv
            SV[0:1, to] += jnp.sum(na * hat, axis=0, keepdims=True)
            SV[1:2, to] += jnp.sum(na, axis=0, keepdims=True)
            SV[2:3, to] += jnp.sum(nm * hat, axis=0, keepdims=True)
            SV[3:4, to] += jnp.sum(nm, axis=0, keepdims=True)
            HP[:, to] = na * gain_attn[:, to] + nm * gain_mlp[:, to]

    blocks = (branch_block, input_block)
    totals = (HB, HP)

    def c_copy(a, k):
        return remote(slot(k % 2), fc_buf.at[a, k], f_ss.at[k % 2], f_rs.at[a, k], dC)

    sent = []

    def fold_over(a, k):
        blocks[a](block_of((3 - k) // 2, (3 - k) % 2, 1))
        for op in [op for op in sent if op[0] == k % 2]:
            op[1].wait_send()
            sent.remove(op)
        slot(k % 2)[...] = totals[a][...].astype(BF16)
        op = c_copy(a, k)
        op.start()
        sent.append((k % 2, op))

    def h_copy(a, w):
        if w < 2:
            src, dst = FS.at[pl.ds(2 * rows + w * half, half)], fh_buf.at[a, w]
        else:
            src, dst = slot(1 + w), fb_buf.at[a, w - 2]
        return remote(src, dst, h_ss.at[w], h_rs.at[a, w], (dX, dY)[w % 2])

    going = {}

    def fold_own(a, k):
        c_copy(a, k).wait_recv()
        get = pltpu.make_async_copy(fc_buf.at[a, k], slot(5), fl.at[0])
        get.start()
        extra = None
        if k in (1, 2):
            w = 2 - k
            h_copy(a, w).wait_recv()
            extra = pltpu.make_async_copy(fh_buf.at[a, w], FS.at[pl.ds(6 * rows, half)], fl.at[1])
            extra.start()
        blocks[a](block_of((3 - k) // 2, (3 - k) % 2, 0))
        get.wait()
        if extra is not None:
            extra.wait()
            at = half if k == 1 else 0
            totals[a][at : at + half] += FS[pl.ds(6 * rows, half)].astype(F32)
        if k < 3:
            which = (0, 1) if k == 0 else (k + 1,)
            for w in which:
                if w in going:
                    going.pop(w).wait_send()
            slot(2 + k)[...] = (totals[a][...] + slot(5)[...].astype(F32)).astype(BF16)
            for w in which:
                going[w] = h_copy(a, w)
                going[w].start()
        else:
            totals[a][...] += slot(5)[...].astype(F32)

    def fold_end(a):
        gets = [pltpu.make_async_copy(fb_buf.at[a, j], slot(5 + j), fl.at[j]) for j in range(2)]
        for j in range(2):
            h_copy(a, 2 + j).wait_recv()
            gets[j].start()
        for get in gets:
            get.wait()

    def own_tiles(a, to_ref, base, body):
        @pl.loop(0, rows // 16)
        def _(t):
            at = ds(t * 16, 16, 16)
            u = (
                totals[a][at]
                + FS[ds(5 * rows + t * 16, 16, 16)].astype(F32)
                + FS[ds(6 * rows + t * 16, 16, 16)].astype(F32)
            )
            to_ref[ds(base + t * 16, 16, 16)] = body(t, at, u).astype(BF16)

    def v_copy(k):
        return remote(SV, SVR.at[k], v_ss.at[k], v_rs.at[k], steps[k])

    keep_row = lax.broadcasted_iota(jnp.int32, (16, 1), 0) < 5

    def small_sums(lo, hi):
        for k in range(lo, hi):
            v_copy(k).start()
            v_copy(k).wait()
            got = SVR[k]
            SV[...] += jnp.where(keep_row, got, 0.0) if k == 2 else got

    hidden_of(0)
    sum_round(2)
    pass_batch(9, 1, 2)
    need(5)
    grad_of(0)
    sum_round(3)
    pass_batch(9, 2, n - 1)

    @pl.loop(1, 3)
    def _(c):
        hidden_of(c)
        sum_round(2 + 2 * c)
        need(5 + 2 * c)
        grad_of(c)
        sum_round(3 + 2 * c)

    hidden_of(3)
    sum_round(8)
    need(UNITS - 1)
    early = n + 2 + LAG <= 8
    if early:
        for k in range(4):
            fold_over(0, k)
    grad_of(3)
    sum_round(9)
    last_round = UNITS + n + LAG - 1
    clear = max(10, n + 3 + LAG)
    if clear > 10:
        @pl.loop(10, clear)
        def _(t):
            sum_round(t)

    rounds = iter(range(clear, last_round))

    def more():
        t = next(rounds, None)
        if t is not None:
            sum_round(t)

    SV[...] = jnp.zeros_like(SV)
    SV[4:5] = jnp.sum(LB[0, ds(own_b * rows, rows, rows)].astype(F32), axis=0, keepdims=True)
    for r in range(3):
        SV[pl.ds(5 + i, 1), r * UNIT : (r + 1) * UNIT] = BQ[r : r + 1]
    for c in range(4):
        SV[pl.ds(5 + i, 1), (3 + c) * UNIT : (4 + c) * UNIT] = BF[c]

    if not early:
        for k in range(4):
            fold_over(0, k)
    more()
    fold_own(0, 0)
    fold_over(1, 0)
    fold_own(1, 0)
    more()
    fold_own(0, 1)
    fold_own(0, 2)
    more()
    fold_over(1, 1)
    fold_over(1, 2)
    fold_own(1, 1)
    fold_own(1, 2)
    more()
    fold_over(1, 3)
    fold_own(0, 3)
    fold_own(1, 3)
    more()

    x_block(own_b).start()
    fold_end(0)
    x_block(own_b).wait()
    bias = b_out[...] + b_proj[...]

    def out_rows(t, at, u):
        live = (own_at + t * 16 < both).astype(F32)
        return XT[at].astype(F32) + live * (u + bias)

    own_tiles(0, XT, 0, out_rows)
    put = pltpu.make_async_copy(XT, out_ref, fl.at[2])
    put.start()
    small_sums(0, len(steps))
    s_gain_a[...] = SV[0:1]
    s_shift_a[...] = SV[1:2]
    s_gain_m[...] = SV[2:3]
    s_shift_m[...] = SV[3:4]
    s_bias[...] = SV[4:5]
    s_bqkv[...] = SV[5 : 5 + INNER, : 3 * UNIT]
    for j in range(INNER):
        s_bfc[:, j * ff : (j + 1) * ff] = SV[5 + j : 6 + j, 3 * UNIT : 3 * UNIT + ff]
    more()

    put.wait()
    x_block(own_b).start()
    for w in list(going):
        going.pop(w).wait_send()
    get = pltpu.make_async_copy(cot, slot(4), fl.at[2])
    get.start()
    fold_end(1)
    x_block(own_b).wait()
    get.wait()

    def grad_rows(t, at, u):
        hat, inv = stats(XT[at].astype(F32))
        return FS[ds(4 * rows + t * 16, 16, 16)].astype(F32) + inv * (
            u - jnp.mean(u, axis=-1, keepdims=True) - hat * jnp.mean(u * hat, axis=-1, keepdims=True)
        )

    own_tiles(1, FS, 7 * rows, grad_rows)
    put = pltpu.make_async_copy(slot(7), gtok_ref, fl.at[2])
    put.start()
    t = next(rounds, None)
    if t is not None:
        @pl.loop(t, last_round)
        def _(t):
            sum_round(t)

    put.wait()

    for p in range(3):
        p_copy(p).wait_send()

    @pl.loop(0, UNITS)
    def _(u):
        for p in range(3):
            o_copy(u, 0, p, go_ref.at[i]).wait_recv()

    for u in range(UNITS):
        for p in range(3):
            a2a_copy(u, p).wait_send()
    for op in xs + cs:
        op.wait_send()

    @pl.loop(0, UNITS)
    def _(u):
        for e in range(2):
            sgn = 1 - 2 * e

            @pl.when((z < n - 1) if e == 0 else (z > 0))
            def _():
                @pl.loop(0, n)
                def _(s):
                    j = z - sgn * s

                    @pl.when((j >= 0) & (j < n))
                    def _():
                        g_copy(u, j, e, s).wait_send()

    for e in range(2):
        @pl.loop(1, n)
        def _(s):
            d = z + (1 - 2 * e) * (n - s)

            @pl.when((d >= 0) & (d < n))
            def _():
                for k in range(DEPTH):
                    r_copy(UNITS - 1 - k, e, s).wait_send()

    for s in range(2):
        o_sent(s)
    for _, op in sent:
        op.wait_send()


def local(
    tokens, lengths, w_qkv, b_qkv, w_out, b_out, w_fc, b_fc, w_proj, b_proj,
    gain_attn, shift_attn, gain_mlp, shift_mlp, cotangent,
):
    n = lax.axis_size("outer")
    rows, width = tokens.shape
    R = w_qkv.shape[0]
    B = INNER * R
    group = rows * lax.axis_size("tensor")
    heads = w_qkv.shape[1]

    lane = np.arange(128)
    freq = np.where(lane < ROT, np.exp((lane % (ROT // 2)) * (2.0 / ROT) * -math.log(10000.0)), 0.0)
    angle = np.arange(group + 8, dtype=np.float32)[:, None] * freq.astype(np.float32)
    tab = jnp.asarray(np.stack([np.cos(angle), np.sin(angle)]).astype(np.float32))

    tall = INNER * group
    n_steps = 3 + max(1, (n - 1).bit_length())
    hbm = pl.BlockSpec(memory_space=pl.ANY)
    vmem = pl.BlockSpec(memory_space=pltpu.VMEM)
    smem = pl.BlockSpec(memory_space=pltpu.SMEM)
    sds = jax.ShapeDtypeStruct
    dma = pltpu.SemaphoreType.DMA
    row = sds((1, width), F32)
    res = pl.pallas_call(
        functools.partial(kernel, n),
        out_shape=(
            sds((rows, width), BF16),
            sds((rows, width), BF16),
            sds((INNER, R, 3 * UNIT), F32),
            sds((INNER, R, UNIT), F32),
            sds(w_fc.shape, F32),
            sds(w_proj.shape, F32),
            row, row, row, row, row,
            sds(b_qkv.shape, F32),
            sds((1,) + b_fc.shape, F32),
            sds((tall, width), BF16),
            sds((UNITS, 2, n - 1, UNIT, B), BF16),
            sds((2, 4, rows, width), BF16),
            sds((2, 2, rows // 2, width), BF16),
            sds((2, 2, rows, width), BF16),
        ),
        in_specs=[hbm] * 2 + [smem] + [hbm] * 5 + [vmem] * 8,
        out_specs=(hbm,) * 6 + (vmem,) * 7 + (hbm,) * 5,
        scratch_shapes=[
            pltpu.VMEM((UNITS, width, UNIT), BF16),
            pltpu.VMEM((3, tall, width), BF16),
            pltpu.VMEM((UNITS, UNIT, tall), BF16),
            pltpu.VMEM((UNIT, tall), F32),
            pltpu.VMEM((rows, width), F32),
            pltpu.VMEM((DEPTH, n - 1, UNIT, B), BF16),
            pltpu.VMEM((2, n - 1, UNIT, B), BF16),
            pltpu.VMEM((2, B, UNIT), F32),
            pltpu.VMEM((rows, width), BF16),
            pltpu.VMEM(tab.shape, F32),
            pltpu.VMEM((8, 128), F32),
            pltpu.VMEM((16, width), F32),
            pltpu.VMEM((n_steps, 16, width), F32),
            pltpu.VMEM((INNER, 8, 128), F32),
            pltpu.VMEM((8, UNIT), F32),
            pltpu.VMEM((4, 1, UNIT), F32),
            dma((3,)), dma((3,)),
            dma((UNITS, 3)), dma((UNITS, 3)), dma((UNITS,)),
            dma((UNITS, 2, n)), dma((UNITS, n)),
            dma((DEPTH, n - 1)), dma((UNITS, 2, n - 1)), dma((2, n - 1)),
            dma((2, 3)), dma((UNITS, 3)), dma((2,)),
            dma((2, 8)), dma((2, 8)), dma((2,)), dma((8,)),
            dma((2,)), dma((2, 4)),
            dma((4,)), dma((2, 4)), dma((3,)),
            dma((n_steps,)), dma((n_steps,)), dma((2,)),
        ],
        compiler_params=pltpu.CompilerParams(
            collective_id=0, has_side_effects=True, vmem_limit_bytes=64 * 1024 * 1024 - 65536
        ),
        name="block",
    )(
        tokens, cotangent, lengths, w_qkv.transpose(1, 0, 2), w_out.transpose(1, 0, 2), w_fc, w_proj, tab,
        b_qkv, b_fc[None], b_out[None], b_proj[None],
        gain_attn[None], shift_attn[None], gain_mlp[None], shift_mlp[None],
    )
    output, grad_tokens, g_qkv, g_out, g_fc, g_proj = res[:6]
    gain_a, shift_a, gain_m, shift_m, bias, bias_qkv, bias_fc = res[6:13]
    return (
        output,
        grad_tokens,
        g_qkv.transpose(1, 0, 2),
        bias_qkv,
        g_out.transpose(1, 0, 2),
        bias[0],
        g_fc,
        bias_fc[0],
        g_proj,
        bias[0],
        gain_a[0],
        shift_a[0],
        gain_m[0],
        shift_m[0],
    )


def solution(mesh):
    n_dp, n_tensor = mesh.devices.shape
    split = Mesh(
        mesh.devices.reshape(n_dp // INNER, INNER, n_tensor), ("outer", "inner", "tensor")
    )
    dp = ("outer", "inner")
    rows = P(("outer", "inner", "tensor"), None)
    w3 = P(dp, "tensor", None)
    w2 = P(dp, "tensor")
    return jax.shard_map(
        local,
        mesh=split,
        in_specs=(
            rows, P(dp, None), w3, P("tensor", None), w3, P(), w2, P("tensor"), w2, P(),
            P(), P(), P(), P(), rows,
        ),
        out_specs=(
            rows, rows, w3, P("tensor", None), w3, P(), w2, P("tensor"), w2, P(), P(), P(), P(), P(),
        ),
        check_vma=False,
    )
```

```python
import functools
import math

import jax
import jax.numpy as jnp
import numpy as np
from jax import lax
from jax.experimental import pallas as pl
from jax.experimental.pallas import tpu as pltpu
from jax.sharding import Mesh
from jax.sharding import PartitionSpec as P

HEAD = 256
ROT = 64
INNER = 4
UNITS = 12
UNIT = 256
DEPTH = 2
F32 = jnp.float32
BF16 = jnp.bfloat16
MESH = pl.DeviceIdType.MESH
NN = (((1,), (0,)), ((), ()))
NT = (((1,), (1,)), ((), ()))
TN = (((0,), (0,)), ((), ()))


PLAN = (
    ("a2a", 0), ("a2a", 3), ("a2a", 1), ("a2a", 5), ("a2a", 2), ("sp1", 0), ("a2a", 4), ("arrive", 0), ("ownm", 0),
    ("arrive", 1), ("ownm", 1), ("arrive", 2), ("ownm", 2), ("a2a", 8), ("arrive", 3), ("sp1", 1), ("pb", 0, 1),
    ("wx", 1, 2), ("a2a", 6), ("ownm", 3), ("a2a", 7), ("a2a", 9), ("sp2", 0), ("sp1", 2), ("arrive", 4),
    ("arrive", 5), ("wx", 0, 2), ("pb", 0, 2), ("ownm", 4), ("sp3", 0), ("sp2", 1), ("ln", 1, "own"),
    ("ln", 0, "own"), ("ln", 0, "xy"), ("ownm", 5), ("wx", 0, 5, 6, 7), ("sp1", 3), ("a2a", 11), ("ln", 1, "xy"),
    ("arrive", 6), ("ln", 0, "dc"), ("need", 0), ("pb", 3, 1), ("sp2", 2), ("arrive", 7), ("ownm", 6), ("sp3", 1),
    ("pb", 3, 2), ("a2a", 10), ("arrive", 8), ("arrive", 9), ("ownm", 7), ("wx", 1, 5, 6, 7), ("ln", 0, "rest"),
    ("sp3", 2), ("need", 1), ("need", 2), ("ownm", 8), ("ln", 1, "dc"), ("sp2", 3), ("ln", 1, "rest"),
    ("af", 2, "a"), ("pb", 6, 1), ("arrive", 10), ("arrive", 11), ("sp3", 3), ("af", 2, "b"), ("ownm", 9),
    ("wx", 3, 2, 5, 6, 7), ("wx", 2, 2, 5, 6, 7), ("E", 0, 1), ("need", 3), ("ab", 2, "a"), ("need", 4),
    ("pb", 6, 2), ("t2", 0), ("E", 0, 2), ("M2", 0), ("E", 0, 3), ("ab", 2, "b"), ("E", 1, 1), ("t3i", 0),
    ("need", 5), ("E", 2, 1), ("M3i", 0), ("E", 1, 2), ("E", 3, 1), ("ownm", 10), ("t2", 1), ("ff", 0),
    ("E", 2, 2), ("t3e", 0), ("E", 1, 3), ("E", 4, 1), ("M2", 1), ("t2", 2), ("E", 2, 3), ("M3e", 0), ("E", 3, 2),
    ("t3i", 1), ("need", 6), ("M2", 2), ("tm", 0), ("t3e", 1), ("M3i", 1), ("t2", 3), ("t3i", 2), ("M3e", 1),
    ("M2", 3), ("ownm", 11), ("ff", 1), ("need", 7), ("E", 5, 1), ("M3i", 2), ("t3e", 2), ("ff", 2), ("t2", 4),
    ("M3e", 2), ("M2", 4), ("Fm", 0), ("E", 4, 2), ("tm", 1), ("ff", 3), ("pb", 9, 1), ("te", 0), ("t3i", 3),
    ("Fe", 0), ("E", 6, 1), ("E", 5, 2), ("M3i", 3), ("t2", 5), ("t3e", 3), ("Fm", 1), ("E", 3, 3), ("t3i", 4),
    ("E", 7, 1), ("M2", 5), ("M3e", 3), ("te", 1), ("Fe", 1), ("te", 2), ("E", 4, 3), ("need", 8), ("M3i", 4),
    ("tm", 2), ("E", 6, 2), ("ff", 4), ("Fe", 2), ("E", 7, 2), ("t2", 6), ("E", 5, 3), ("E", 8, 1), ("te", 3),
    ("t3e", 4), ("Fe", 3), ("Fm", 2), ("pb", 9, 2), ("M2", 6), ("M3e", 4), ("tm", 3), ("need", 9), ("ff", 5),
    ("t3i", 5), ("E", 6, 3), ("E", 9, 1), ("need", 10), ("Fm", 3), ("t3e", 5), ("ff", 6), ("need", 11), ("M3i", 5),
    ("t2", 7), ("A", 0, 0), ("ff", 7), ("t3i", 6), ("E", 8, 2), ("M3e", 5), ("E", 7, 3), ("M2", 7), ("B", 0, 0),
    ("E", 9, 2), ("te", 4), ("tm", 4), ("A", 1, 0), ("t3e", 6), ("Fm", 4), ("M3i", 6), ("A", 0, 1), ("M3e", 6),
    ("Fe", 4), ("t2", 8), ("E", 10, 1), ("B", 1, 0), ("t3e", 7), ("A", 0, 2), ("M2", 8), ("M3e", 7), ("t3i", 7),
    ("tm", 5), ("B", 0, 1), ("te", 5), ("E", 8, 3), ("A", 1, 1), ("Fe", 5), ("te", 6), ("B", 0, 2), ("A", 0, 3),
    ("t3e", 8), ("Fm", 5), ("E", 11, 1), ("A", 1, 3), ("M3i", 7), ("M3e", 8), ("E", 10, 2), ("Fe", 6), ("t2", 9),
    ("E", 9, 3), ("t3i", 8), ("tm", 6), ("A", 1, 2), ("M2", 9), ("M3i", 8), ("t3i", 9), ("Fm", 6), ("E", 11, 2),
    ("te", 7), ("B", 1, 1), ("t2", 10), ("M2", 10), ("E", 10, 3), ("t3e", 9), ("tm", 7), ("B", 1, 2), ("Fm", 7),
    ("tm", 8), ("t2", 11), ("M3i", 9), ("t3i", 10), ("M3e", 9), ("B", 0, 3), ("B", 1, 3), ("t3e", 10), ("vs", 0),
    ("C", 0), ("M2", 11), ("vs", 1), ("M3e", 10), ("Fe", 7), ("Fm", 8), ("tm", 9), ("te", 8), ("M3i", 10),
    ("own", 0), ("Fe", 8), ("te", 9), ("t3i", 11), ("E", 11, 3), ("Fm", 9), ("t3e", 11), ("M3i", 11), ("Fe", 9),
    ("vs", 2), ("M3e", 11), ("te", 10), ("tm", 10), ("Fe", 10), ("te", 11), ("Fm", 10), ("vs", 3), ("tm", 11),
    ("C", 1), ("Fe", 11), ("vs", 4), ("own", 1), ("Fm", 11), ("vs", 5),
)


def dot(a, b, dims=NN):
    return lax.dot_general(a, b, dims, preferred_element_type=F32)


def kernel(
    n, tokens, cot, lens, wq, wo, w_fc, w_proj, tab, b_qkv, b_fc, b_out, b_proj,
    gain_attn, shift_attn, gain_mlp, shift_mlp,
    out_ref, gtok_ref, gq_ref, go_ref, gfc_ref, gpj_ref,
    s_gain_a, s_shift_a, s_gain_m, s_shift_m, s_bias, s_bqkv, s_bfc,
    xa, rbuf, fc_buf, fh_buf, fb_buf,
    W, LB, RT, HP, HB, STG, INB, FIN, XT, TAB, PAY, SV, SVR, LENB, BQ, BF,
    p_ss, p_rs, a_ss, a_rs, a_ls, g_ss, g_rs, r_ss, r_rs, r_ls, o_ss, o_rs, o_ls,
    x_ss, x_rs, x_ls, l_ls, f_ss, f_rs, h_ss, h_rs, fl, v_ss, v_rs, loc,
):
    z = lax.axis_index("outer")
    i = lax.axis_index("inner")
    y = lax.axis_index("tensor")
    rows, width = tokens.shape
    B = width // n
    R = B // INNER
    group = 2 * rows
    groups = INNER
    ff = UNIT * 4
    ends = z // (n - 1) + (n - 1 - z) // (n - 1)
    mid = (z > 0) & (z < n - 1)
    iC = i + 1 - 2 * lax.rem(i, 2)
    iX = lax.rem(i + 2, INNER)
    iXC = INNER - 1 - i
    inner_peers = (iC, iX, iXC)
    dC, dX, dY = {"inner": iC}, {"inner": iX}, {"tensor": 1 - y}
    steps = [dC, dX, dY]
    k = 1
    while k < n:
        steps.append({"outer": z + k * (1 - 2 * lax.rem(z // k, 2))})
        k *= 2

    def ds(start, size, mult):
        return pl.ds(pl.multiple_of(start, mult), size)

    def remote(src, dst, ss, rs, dev):
        return pltpu.make_async_remote_copy(
            src_ref=src, dst_ref=dst, send_sem=ss, recv_sem=rs, device_id=dev, device_id_type=MESH
        )

    bar = pltpu.get_barrier_semaphore()
    greet = steps[:3] + [{"inner": iXC}] + steps[4:]
    for dev in greet:
        pl.semaphore_signal(bar, inc=1, device_id=dev, device_id_type=MESH)

    @pl.when(z > 0)
    def _():
        pl.semaphore_signal(bar, inc=1, device_id={"outer": z - 1}, device_id_type=MESH)

    @pl.when(z < n - 1)
    def _():
        pl.semaphore_signal(bar, inc=1, device_id={"outer": z + 1}, device_id_type=MESH)

    pl.semaphore_wait(bar, len(greet) + (z + n - 1) // n + (2 * n - 2 - z) // n)

    def piece(u, to):
        if u < 3:
            return wq.at[to, :, pl.ds(u * UNIT, UNIT)]
        if u == 3:
            return wo.at[to]
        ref = (w_fc, w_proj)[u % 2]
        return ref.at[:, ds(to * ff + (u - 4) // 2 * UNIT, UNIT, UNIT)]

    def a2a_copy(u, p):
        dst = W.at[u, ds(z * B + i * R, R, R)]
        return remote(
            piece(u, inner_peers[p]), dst, a_ss.at[u, p], a_rs.at[u, p], {"inner": inner_peers[p]}
        )

    def a2a_own(u):
        return pltpu.make_async_copy(piece(u, i), W.at[u, ds(z * B + i * R, R, R)], a_ls.at[u])

    def a2a(*units):
        for u in units:
            for p in (1, 2, 0):
                a2a_copy(u, p).start()
            a2a_own(u).start()

    def g_copy(u, j, e, s):
        blk = W.at[u, ds(j * B, B, B)]
        return remote(blk, blk, g_ss.at[u, e, s], g_rs.at[u, j], {"outer": z + 1 - 2 * e})

    def send_own(u):
        for e in range(2):
            @pl.when((z < n - 1) if e == 0 else (z > 0))
            def _():
                g_copy(u, z, e, 0).start()

    def arrive(*units):
        for u in units:
            for p in range(3):
                a2a_copy(u, p).wait_recv()
            a2a_own(u).wait()

            @pl.when(ends > 0)
            def _():
                send_own(u)

    def own_batch(*units):
        @pl.when(mid)
        def _():
            for u in units:
                send_own(u)

    def pass_on(u, s):
        for e in range(2):
            sgn = 1 - 2 * e
            j = z - sgn * s

            @pl.when((j >= 0) & (j < n))
            def _():
                g_copy(u, j, e, s).wait_recv()

                @pl.when((z < n - 1) if e == 0 else (z > 0))
                def _():
                    g_copy(u, j, e, s).start()

    def pass_batch(first, lo, hi):
        @pl.when(mid)
        def _():
            @pl.loop(lo, hi)
            def _(s):
                @pl.loop(first, first + 3)
                def _(u):
                    pass_on(u, s)

    def need(u):
        @pl.when(ends > 0)
        def _():
            @pl.loop(1, n)
            def _(s):
                pass_on(u, s)

    def left(v):
        return 0 if v == 0 else 1 if v < 4 else v % 2 * 2

    def stage(e, s):
        return (1 - e) * (s - 1) + e * (n - 1 - s)

    def r_copy(v, e, s):
        at, k = v % DEPTH, stage(e, s)
        return remote(
            STG.at[at, k], rbuf.at[v, e, s - 1], r_ss.at[at, k], r_rs.at[v, e, s - 1],
            {"outer": z + 1 - 2 * e},
        )

    def r_load(v, e, s):
        return pltpu.make_async_copy(rbuf.at[v, e, s - 1], INB.at[e, s - 1], r_ls.at[e, s - 1])

    def partial(v, d):
        return dot(RT[v], LB[left(v), :, ds(d * B, B, 128)])

    def send_sum(v, e, s, val):
        if v >= DEPTH:
            r_copy(v, e, s).wait_send()
        STG[v % DEPTH, stage(e, s)] = val.astype(BF16)
        r_copy(v, e, s).start()

    def fetch(v, e, s):
        r_copy(v, e, s - 1).wait_recv()
        r_load(v, e, s - 1).start()

    def ends_send(v, k):
        lo, hi = (1, n - 2) if k == 1 else (n - 4 + k, n - 3 + k)

        @pl.when(ends > 0)
        def _():
            e = z // (n - 1)

            @pl.loop(lo, hi)
            def _(s):
                send_sum(v, e, s, partial(v, z + (1 - 2 * e) * (n - s)))

    def mid_steps(lo, hi, body):
        @pl.when(mid)
        def _():
            @pl.loop(lo, hi)
            def _(s):
                @pl.loop(0, 2)
                def _(e):
                    d = z + (1 - 2 * e) * (n - s)

                    @pl.when((d >= 0) & (d < n))
                    def _():
                        body(e, s, d)

    def mid_fetch(v, s):
        mid_steps(s, s + 1, lambda e, s, d: fetch(v, e, s))

    def add_and_send(v, e, s, d):
        r_load(v, e, s - 1).wait()
        send_sum(v, e, s, partial(v, d) + INB[e, s - 2].astype(F32))

    def mid_send(v):
        def body(e, s, d):
            if n != 4:
                fetch(v, e, s)
            add_and_send(v, e, s, d)

        mid_steps(2, n - 1, body)

    def last_way(outward):
        e = z // (n // 2)
        return 1 - e if outward else e

    def last_fetch(v, outward):
        @pl.when(mid)
        def _():
            fetch(v, last_way(outward), n - 1)

    def last_send(v, outward):
        @pl.when(mid)
        def _():
            e = last_way(outward)
            add_and_send(v, e, n - 1, z + 1 - 2 * e)

    def end_fetch(v):
        @pl.when(ends > 0)
        def _():
            fetch(v, 1 - z // (n - 1), n)

    def o_copy(v, slot, p, dst):
        if p == 3:
            return pltpu.make_async_copy(FIN.at[slot, ds(i * R, R, R)], dst, o_ls.at[slot])
        src = FIN.at[slot, ds(inner_peers[p] * R, R, R)]
        return remote(src, dst, o_ss.at[slot, p], o_rs.at[v, p], {"inner": inner_peers[p]})

    def o_sent(slot):
        for p in range(3):
            o_copy(0, slot, p, go_ref.at[i]).wait_send()
        o_copy(0, slot, 3, go_ref.at[i]).wait()

    def finish(v, total):
        slot = v % 2
        if v > 1:
            o_sent(slot)
        FIN[slot] = total.T.astype(BF16)
        at = ds(i * ff + (v - 4) // 2 * UNIT, UNIT, UNIT) if v >= 4 else None
        if v == 0:
            dst = go_ref.at[i]
        elif v < 4:
            dst = gq_ref.at[i, :, pl.ds((v - 1) * UNIT, UNIT)]
        else:
            dst = (gpj_ref, gfc_ref)[v % 2].at[:, at]
        for p in (1, 2, 0, 3):
            o_copy(v, slot, p, dst).start()

    def mid_finish(v):
        @pl.when(mid)
        def _():
            for e in range(2):
                r_load(v, e, n - 1).wait()
            finish(v, partial(v, z) + INB[0, n - 2].astype(F32) + INB[1, n - 2].astype(F32))

    def end_finish(v):
        @pl.when(ends > 0)
        def _():
            e = 1 - z // (n - 1)
            r_load(v, e, n - 1).wait()
            finish(v, partial(v, z) + INB[e, n - 2].astype(F32))

    def block_of(fx, fy, fc):
        at = lax.rem(i + 2 * fx, INNER)
        at = at + fc * (1 - 2 * lax.rem(at, 2))
        return at * 2 + lax.rem(y + fy, 2)

    def block_rows(k):
        return block_of(lax.rem(k, 2), lax.rem(k // 2, 2), k // 4)

    half = rows // 2

    def part(ref, b, which=None):
        if which is None:
            return ref.at[ds(b * rows, rows, rows)]
        return ref.at[ds(b * rows + which * half, half, half)]

    own_b, x_b, y_b, d_b = (block_of(a, b, 0) for a, b in ((0, 0), (1, 0), (0, 1), (1, 1)))

    def x_sends(a, h, src, dst):
        def mk(k, s, d, dev):
            return remote(s, d, x_ss.at[a, k], x_rs.at[a, k], dev)

        way, on = ((dY, x_b), (dX, y_b))[h]
        return [
            mk(0, src, part(dst, own_b, h), dX),
            mk(1, src, part(dst, own_b, h), dY),
            mk(2, src, part(dst, own_b, h), dC),
            mk(3, part(dst, on, h), part(dst, on, h), way),
            None,
            mk(5, part(dst, x_b, h), part(dst, x_b, h), dC),
            mk(6, part(dst, y_b, h), part(dst, y_b, h), dC),
            mk(7, part(dst, d_b, h), part(dst, d_b, h), dC),
        ]

    gb_ref = LB.at[0]
    xs = [x_sends(h, h, tokens.at[pl.ds(h * half, half)], xa) for h in range(2)]
    xs += [x_sends(2 + h, h, part(gb_ref, own_b, h), gb_ref) for h in range(2)]
    x_local = pltpu.make_async_copy(tokens, part(xa, own_b), x_ls.at[0])
    c_local = pltpu.make_async_copy(cot, part(gb_ref, own_b), x_ls.at[1])

    def near(h, k, src=None):
        b = block_rows(k)
        return pltpu.make_async_copy(
            part(xa, b, h) if src is None else src.at[pl.ds(h * half, half)], part(LB.at[2], b, h), l_ls.at[h, k]
        )

    def spread_first(a):
        for k in (1, 0, 2):
            xs[a][k].start()

    def spread_second(a):
        for k in (0, 1) if a % 2 == 0 else (1, 0):
            xs[a][k].wait_recv()
            if k == a % 2:
                xs[a][3].start()
            xs[a][5 + k].start()

    def spread_third(a):
        xs[a][3].wait_recv()
        xs[a][7].start()

    def stats(v):
        center = v - jnp.mean(v, axis=-1, keepdims=True)
        inv = lax.rsqrt(jnp.mean(center * center, axis=-1, keepdims=True) + 1e-05)
        return center * inv, inv

    def norm_block(h, k):
        b = block_rows(k)
        near(h, k).wait()

        @pl.loop(0, half // 16)
        def _(t):
            to = ds(b * rows + h * half + t * 16, 16, 16)
            hat, _ = stats(LB[2, to].astype(F32))
            LB[1, to] = (hat * gain_attn[...] + shift_attn[...]).astype(BF16)
            LB[2, to] = (hat * gain_mlp[...] + shift_mlp[...]).astype(BF16)

    def p_copy(p):
        return remote(PAY, LENB.at[i], p_ss.at[p], p_rs.at[p], {"inner": inner_peers[p]})

    tab_in = pltpu.make_async_copy(tab, TAB, loc.at[0])
    p_own = pltpu.make_async_copy(PAY, LENB.at[i], loc.at[1])
    first = lens[0, 0]
    both = first + lens[0, 1]
    own_at = y * rows + lax.broadcasted_iota(jnp.int32, (16, 1), 0)

    def lengths_out():
        x_local.start()
        for h in range(2):
            near(h, 0, tokens).start()
        c_local.start()
        BQ[...] = jnp.zeros_like(BQ)
        BF[...] = jnp.zeros_like(BF)
        SV[...] = jnp.zeros_like(SV)
        tab_in.wait()
        for k, at in enumerate((first, both)):
            for h in range(2):
                PAY[2 * k + h : 2 * k + h + 1] = TAB[h, pl.ds(at, 1)]
            PAY[4 + k : 5 + k] = jnp.full((1, 128), at.astype(F32))
        PAY[6:8] = jnp.zeros((2, 128), F32)
        for p in range(3):
            p_copy(p).start()
        p_own.start()

    def lengths_in():
        for p in range(3):
            p_copy(p).wait_recv()
        p_own.wait()

    def rows_out(a):
        if a == 2:
            c_local.wait()

            @pl.loop(0, rows // 16)
            def _(t):
                to = ds(own_b * rows + t * 16, 16, 16)
                live = own_at + t * 16 < both
                LB[0, to] = jnp.where(live, LB[0, to].astype(F32), 0.0).astype(BF16)

        spread_first(a)

    def rows_on(a):
        spread_second(a)
        if a < 2:
            near(a, 1).start()
            near(a, 2).start()

    def rows_last(a):
        spread_third(a)
        if a < 2:
            near(a, 3).start()

    def rows_in(a, *ks):
        for k in ks:
            xs[a][k].wait_recv()
            if a < 2:
                near(a, {2: 4}.get(k, k)).start()
        if a == 0 and ks[0] == 2:
            x_local.wait()

    def norms(h, which):
        for k in {"own": (0,), "xy": (1, 2), "dc": (3, 4)}.get(which, ()):
            norm_block(h, k)
        if which == "rest":
            @pl.loop(5, 8)
            def _(k):
                norm_block(h, k)

    scale = 1.0 / math.sqrt(HEAD)
    lane = lax.broadcasted_iota(jnp.int32, (group, 128), 1)
    row_at = lax.broadcasted_iota(jnp.int32, (group, 1), 0).astype(F32)
    q_at = lax.broadcasted_iota(jnp.int32, (group, group), 0)
    k_at = lax.broadcasted_iota(jnp.int32, (group, group), 1)

    def turning(g):
        info = LENB[g]
        a, ab = info[4:5, 0:1], info[5:6, 0:1]
        in_a = row_at < a
        in_b = row_at < ab
        ca = jnp.where(in_a, 1.0, jnp.where(in_b, info[0:1], info[2:3]))
        sa = jnp.where(in_a, 0.0, jnp.where(in_b, info[1:2], info[3:4]))
        tcos, tsin = TAB[0, :group], TAB[1, :group]
        cosine = tcos * ca + tsin * sa
        sine = tsin * ca - tcos * sa
        low = jnp.where(lane < ROT // 2, -sine, 0.0)
        high = jnp.where(lane < ROT // 2, 0.0, sine)
        begin = jnp.where(in_a, 0.0, jnp.where(in_b, a, ab)).astype(jnp.int32)
        return cosine, low, high, begin

    def turn(v, cosine, low, high):
        first = v[:, :128]
        first = (
            first * cosine
            + pltpu.roll(first, 128 - ROT // 2, 1) * low
            + pltpu.roll(first, ROT // 2, 1) * high
        )
        return jnp.concatenate([first, v[:, 128:]], axis=1)

    def keep(slot, g, v):
        for h in range(group // 256):
            RT[slot, :, ds(g * group + h * 256, 256, 256)] = v[h * 256 : (h + 1) * 256]

    def kept(slot, g):
        return jnp.concatenate(
            [RT[slot, :, ds(g * group + h * 256, 256, 256)] for h in range(group // 256)], axis=0
        )

    def softmax(q, kk, begin):
        scores = dot(q, kk, NT) * scale
        allowed = (k_at <= q_at) & (k_at >= begin)
        scores = jnp.where(allowed, scores, -1e30)
        shifted = jnp.exp(scores - jnp.max(scores, axis=-1, keepdims=True))
        return shifted / jnp.sum(shifted, axis=-1, keepdims=True)

    def attend(lo, hi):
        @pl.loop(lo, hi)
        def _(g):
            at = ds(g * group, group, group)
            cosine, low, high, begin = turning(g)
            nm = LB[1, at]
            bias = [b_qkv[pl.ds(i, 1), r * UNIT : (r + 1) * UNIT] for r in range(3)]
            q = turn(dot(nm, W[0]) + bias[0], cosine, low, high).astype(BF16)
            keep(4, g, q)
            kk = turn(dot(nm, W[1]) + bias[1], cosine, low, high).astype(BF16)
            keep(5, g, kk)
            vv = (dot(nm, W[2]) + bias[2]).astype(BF16)
            keep(6, g, vv)
            probs = softmax(q, kk, begin).astype(BF16)
            mixed = dot(probs, vv).astype(BF16)
            RT[0, :, at] = mixed.T

    def attend_back(lo, hi):
        @pl.loop(lo, hi)
        def _(g):
            at = ds(g * group, group, group)
            cosine, low, high, begin = turning(g)
            q, kk, vv = kept(4, g), kept(5, g), kept(6, g)
            probs = softmax(q, kk, begin)
            gm = dot(LB[0, at], W[3]).astype(BF16)
            gp = dot(gm, vv, NT)
            gs = (probs * (gp - jnp.sum(probs * gp, axis=-1, keepdims=True))).astype(BF16)
            gv = dot(probs.astype(BF16), gm, TN).astype(BF16)
            gq = turn(dot(gs, kk) * scale, cosine, -low, -high).astype(BF16)
            gk = turn(dot(gs, q, TN) * scale, cosine, -low, -high).astype(BF16)
            for r, val in enumerate((gq, gk, gv)):
                RT[1 + r, :, at] = val.T
                BQ[r : r + 1] += jnp.sum(val.astype(F32), axis=0, keepdims=True)

    def hidden_of(c):
        u = 4 + 2 * c

        @pl.loop(0, groups)
        def _(g):
            at = ds(g * group, group, group)
            pre = dot(LB[2, at], W[u]) + b_fc[:, ds(i * ff + c * UNIT, UNIT, UNIT)]
            phi = 0.5 * (1.0 + lax.erf(pre * (1.0 / math.sqrt(2.0))))
            slope = phi + pre * jnp.exp(-0.5 * pre * pre) * (1.0 / math.sqrt(2.0 * math.pi))
            for h in range(group // 256):
                HP[:, ds(g * group + h * 256, 256, 256)] = slope[h * 256 : (h + 1) * 256]
            RT[u, :, at] = (pre * phi).astype(BF16).T

    def grad_of(c):
        u = 4 + 2 * c

        @pl.loop(0, groups)
        def _(g):
            at = ds(g * group, group, group)
            gh = dot(LB[0, at], W[u + 1])
            slope = jnp.concatenate(
                [HP[:, ds(g * group + h * 256, 256, 256)] for h in range(group // 256)], axis=0
            )
            val = (gh * slope).astype(BF16)
            BF[c] += jnp.sum(val.astype(F32), axis=0, keepdims=True)
            RT[u + 1, :, at] = val.T

    FS = LB.at[1]
    wide = 512
    tiles = width // wide

    def slot(k):
        return FS.at[pl.ds(k * rows, rows)]

    LT = FS.at[pl.ds(7 * rows, rows)]

    def side(us, to):
        return jnp.concatenate([W[u, to] for u in us], axis=1)

    def turn_left(b, vs):
        at = ds(b * rows, rows, rows)
        for k, v in enumerate(vs):
            LT[:, k * UNIT : (k + 1) * UNIT] = RT[v, :, at].T

    def branch_block(b):
        turn_left(b, (0, 4, 6, 8, 10))

        @pl.loop(0, tiles)
        def _(t):
            to = ds(t * wide, wide, wide)
            HB[:, to] = dot(LT[:, : 5 * UNIT], side((3, 5, 7, 9, 11), to), NT)

    def x_block(b):
        return pltpu.make_async_copy(part(xa, b), XT, loc.at[0])

    def input_block(b):
        x_block(b).start()
        turn_left(b, (1, 2, 3, 5, 7, 9, 11))
        x_block(b).wait()
        v = XT[...].astype(F32)
        mean = jnp.mean(v, axis=-1, keepdims=True)
        center = v - mean
        inv = lax.rsqrt(jnp.mean(center * center, axis=-1, keepdims=True) + 1e-05)

        @pl.loop(0, tiles)
        def _(t):
            to = ds(t * wide, wide, wide)
            na = dot(LT[:, : 3 * UNIT], side((0, 1, 2), to), NT)
            nm = dot(LT[:, 3 * UNIT : 7 * UNIT], side((4, 6, 8, 10), to), NT)
            hat = (XT[:, to].astype(F32) - mean) * inv
            SV[0:1, to] += jnp.sum(na * hat, axis=0, keepdims=True)
            SV[1:2, to] += jnp.sum(na, axis=0, keepdims=True)
            SV[2:3, to] += jnp.sum(nm * hat, axis=0, keepdims=True)
            SV[3:4, to] += jnp.sum(nm, axis=0, keepdims=True)
            HP[:, to] = na * gain_attn[:, to] + nm * gain_mlp[:, to]

    blocks = (branch_block, input_block)
    totals = (HB, HP)

    def c_copy(a, k):
        return remote(slot(k % 2), fc_buf.at[a, k], f_ss.at[k % 2], f_rs.at[a, k], dC)

    sent = []

    def fold_over(a, k):
        blocks[a](block_of((3 - k) // 2, (3 - k) % 2, 1))
        for op in [op for op in sent if op[0] == k % 2]:
            op[1].wait_send()
            sent.remove(op)
        slot(k % 2)[...] = totals[a][...].astype(BF16)
        op = c_copy(a, k)
        op.start()
        sent.append((k % 2, op))

    def h_copy(a, w):
        if w < 2:
            src, dst = FS.at[pl.ds(2 * rows + w * half, half)], fh_buf.at[a, w]
        else:
            src, dst = slot(1 + w), fb_buf.at[a, w - 2]
        return remote(src, dst, h_ss.at[w], h_rs.at[a, w], (dX, dY)[w % 2])

    going = {}

    def fold_own(a, k):
        c_copy(a, k).wait_recv()
        get = pltpu.make_async_copy(fc_buf.at[a, k], slot(5), fl.at[0])
        get.start()
        extra = None
        if k in (1, 2):
            w = 2 - k
            h_copy(a, w).wait_recv()
            extra = pltpu.make_async_copy(fh_buf.at[a, w], FS.at[pl.ds(6 * rows, half)], fl.at[1])
            extra.start()
        blocks[a](block_of((3 - k) // 2, (3 - k) % 2, 0))
        get.wait()
        if extra is not None:
            extra.wait()
            at = half if k == 1 else 0
            totals[a][at : at + half] += FS[pl.ds(6 * rows, half)].astype(F32)
        if k < 3:
            which = (0, 1) if k == 0 else (k + 1,)
            for w in which:
                if w in going:
                    going.pop(w).wait_send()
            slot(2 + k)[...] = (totals[a][...] + slot(5)[...].astype(F32)).astype(BF16)
            for w in which:
                going[w] = h_copy(a, w)
                going[w].start()
        else:
            totals[a][...] += slot(5)[...].astype(F32)

    def fold_end(a):
        gets = [pltpu.make_async_copy(fb_buf.at[a, j], slot(5 + j), fl.at[j]) for j in range(2)]
        for j in range(2):
            h_copy(a, 2 + j).wait_recv()
            gets[j].start()
        for get in gets:
            get.wait()

    def own_tiles(a, to_ref, base, body):
        @pl.loop(0, rows // 16)
        def _(t):
            at = ds(t * 16, 16, 16)
            u = (
                totals[a][at]
                + FS[ds(5 * rows + t * 16, 16, 16)].astype(F32)
                + FS[ds(6 * rows + t * 16, 16, 16)].astype(F32)
            )
            to_ref[ds(base + t * 16, 16, 16)] = body(t, at, u).astype(BF16)

    def v_copy(k):
        return remote(SV, SVR.at[k], v_ss.at[k], v_rs.at[k], steps[k])

    keep_row = lax.broadcasted_iota(jnp.int32, (16, 1), 0) < 5

    def small_take(k):
        v_copy(k).wait()
        got = SVR[k]
        SV[...] += jnp.where(keep_row, got, 0.0) if k == 2 else got

    def small_sums(k):
        if k == 0:
            SV[4:5] = jnp.sum(LB[0, ds(own_b * rows, rows, rows)].astype(F32), axis=0, keepdims=True)
            for r in range(3):
                SV[pl.ds(5 + i, 1), r * UNIT : (r + 1) * UNIT] = BQ[r : r + 1]
            for c in range(4):
                SV[pl.ds(5 + i, 1), (3 + c) * UNIT : (4 + c) * UNIT] = BF[c]
        else:
            small_take(k - 1)
        if k < 5:
            v_copy(k).start()
            return
        for m in range(5, len(steps)):
            v_copy(m).start()
            small_take(m)
        s_gain_a[...] = SV[0:1]
        s_shift_a[...] = SV[1:2]
        s_gain_m[...] = SV[2:3]
        s_shift_m[...] = SV[3:4]
        s_bias[...] = SV[4:5]
        s_bqkv[...] = SV[5 : 5 + INNER, : 3 * UNIT]
        for j in range(INNER):
            s_bfc[:, j * ff : (j + 1) * ff] = SV[5 + j : 6 + j, 3 * UNIT : 3 * UNIT + ff]

    def own_out():
        x_block(own_b).start()
        x_block(own_b).wait()
        bias = b_out[...] + b_proj[...]

        def body(t, at, u):
            live = (own_at + t * 16 < both).astype(F32)
            return XT[at].astype(F32) + live * (u + bias)

        own_tiles(0, XT, 0, body)
        put_out.start()

    def own_grad():
        put_out.wait()
        x_block(own_b).start()
        for w in list(going):
            going.pop(w).wait_send()
        get = pltpu.make_async_copy(cot, slot(4), fl.at[2])
        get.start()
        x_block(own_b).wait()
        get.wait()

        def body(t, at, u):
            hat, inv = stats(XT[at].astype(F32))
            return FS[ds(4 * rows + t * 16, 16, 16)].astype(F32) + inv * (
                u - jnp.mean(u, axis=-1, keepdims=True) - hat * jnp.mean(u * hat, axis=-1, keepdims=True)
            )

        own_tiles(1, FS, 7 * rows, body)
        put_grad.start()

    put_out = pltpu.make_async_copy(XT, out_ref, fl.at[2])
    put_grad = pltpu.make_async_copy(slot(7), gtok_ref, fl.at[2])

    def own_rows(a):
        (own_out, own_grad)[a]()

    def ff_half(r):
        (hidden_of, grad_of)[r % 2](r // 2)

    ops = {
        "a2a": a2a,
        "arrive": arrive,
        "ownm": own_batch,
        "pb": lambda f, s: pass_batch(f, 1, 2) if s == 1 else pass_batch(f, 2, n - 1),
        "need": need,
        "sp1": rows_out,
        "sp2": rows_on,
        "sp3": rows_last,
        "wx": rows_in,
        "ln": norms,
        "af": lambda c, h: attend(*((0, groups // 2) if h == "a" else (groups // 2, groups))),
        "ab": lambda c, h: attend_back(*((0, groups // 2) if h == "a" else (groups // 2, groups))),
        "ff": ff_half,
        "E": ends_send,
        "t2": lambda v: mid_fetch(v, 2) if n == 4 else None,
        "M2": mid_send,
        "t3i": lambda v: last_fetch(v, False),
        "t3e": lambda v: last_fetch(v, True),
        "M3i": lambda v: last_send(v, False),
        "M3e": lambda v: last_send(v, True),
        "tm": lambda v: mid_fetch(v, n),
        "Fm": mid_finish,
        "te": end_fetch,
        "Fe": end_finish,
        "A": fold_over,
        "B": fold_own,
        "C": fold_end,
        "own": own_rows,
        "vs": small_sums,
    }
    tab_in.start()
    for op in PLAN:
        if op == ("af", 2, "a"):
            lengths_in()
        ops[op[0]](*op[1:])
        if op == ("sp1", 0):
            lengths_out()
    put_grad.wait()

    for p in range(3):
        p_copy(p).wait_send()

    @pl.loop(0, UNITS)
    def _(u):
        for p in range(3):
            o_copy(u, 0, p, go_ref.at[i]).wait_recv()

    for u in range(UNITS):
        for p in range(3):
            a2a_copy(u, p).wait_send()
    for op in sum(xs, []):
        if op is not None:
            op.wait_send()

    @pl.loop(0, UNITS)
    def _(u):
        for e in range(2):
            sgn = 1 - 2 * e

            @pl.when((z < n - 1) if e == 0 else (z > 0))
            def _():
                @pl.loop(0, n)
                def _(s):
                    j = z - sgn * s

                    @pl.when((j >= 0) & (j < n))
                    def _():
                        g_copy(u, j, e, s).wait_send()

    for e in range(2):
        @pl.loop(1, n)
        def _(s):
            d = z + (1 - 2 * e) * (n - s)

            @pl.when((d >= 0) & (d < n))
            def _():
                for k in range(DEPTH):
                    r_copy(UNITS - 1 - k, e, s).wait_send()

    for s in range(2):
        o_sent(s)
    for _, op in sent:
        op.wait_send()


def local(
    tokens, lengths, w_qkv, b_qkv, w_out, b_out, w_fc, b_fc, w_proj, b_proj,
    gain_attn, shift_attn, gain_mlp, shift_mlp, cotangent,
):
    n = lax.axis_size("outer")
    rows, width = tokens.shape
    R = w_qkv.shape[0]
    B = INNER * R
    group = rows * lax.axis_size("tensor")

    lane = np.arange(128)
    freq = np.where(lane < ROT, np.exp((lane % (ROT // 2)) * (2.0 / ROT) * -math.log(10000.0)), 0.0)
    angle = np.arange(group + 8, dtype=np.float32)[:, None] * freq.astype(np.float32)
    tab = jnp.asarray(np.stack([np.cos(angle), np.sin(angle)]).astype(np.float32))

    tall = INNER * group
    n_steps = 3 + max(1, (n - 1).bit_length())
    hbm = pl.BlockSpec(memory_space=pl.ANY)
    vmem = pl.BlockSpec(memory_space=pltpu.VMEM)
    smem = pl.BlockSpec(memory_space=pltpu.SMEM)
    sds = jax.ShapeDtypeStruct
    dma = pltpu.SemaphoreType.DMA
    row = sds((1, width), F32)
    res = pl.pallas_call(
        functools.partial(kernel, n),
        out_shape=(
            sds((rows, width), BF16),
            sds((rows, width), BF16),
            sds((INNER, R, 3 * UNIT), BF16),
            sds((INNER, R, UNIT), BF16),
            sds(w_fc.shape, BF16),
            sds(w_proj.shape, BF16),
            row, row, row, row, row,
            sds(b_qkv.shape, F32),
            sds((1,) + b_fc.shape, F32),
            sds((tall, width), BF16),
            sds((UNITS, 2, n - 1, UNIT, B), BF16),
            sds((2, 4, rows, width), BF16),
            sds((2, 2, rows // 2, width), BF16),
            sds((2, 2, rows, width), BF16),
        ),
        in_specs=[hbm] * 2 + [smem] + [hbm] * 5 + [vmem] * 8,
        out_specs=(hbm,) * 6 + (vmem,) * 7 + (hbm,) * 5,
        scratch_shapes=[
            pltpu.VMEM((UNITS, width, UNIT), BF16),
            pltpu.VMEM((3, tall, width), BF16),
            pltpu.VMEM((UNITS, UNIT, tall), BF16),
            pltpu.VMEM((UNIT, tall), F32),
            pltpu.VMEM((rows, width), F32),
            pltpu.VMEM((DEPTH, n - 1, UNIT, B), BF16),
            pltpu.VMEM((2, n - 1, UNIT, B), BF16),
            pltpu.VMEM((2, B, UNIT), BF16),
            pltpu.VMEM((rows, width), BF16),
            pltpu.VMEM(tab.shape, F32),
            pltpu.VMEM((8, 128), F32),
            pltpu.VMEM((16, width), F32),
            pltpu.VMEM((n_steps, 16, width), F32),
            pltpu.VMEM((INNER, 8, 128), F32),
            pltpu.VMEM((8, UNIT), F32),
            pltpu.VMEM((4, 1, UNIT), F32),
            dma((3,)), dma((3,)),
            dma((UNITS, 3)), dma((UNITS, 3)), dma((UNITS,)),
            dma((UNITS, 2, n)), dma((UNITS, n)),
            dma((DEPTH, n - 1)), dma((UNITS, 2, n - 1)), dma((2, n - 1)),
            dma((2, 3)), dma((UNITS, 3)), dma((2,)),
            dma((4, 8)), dma((4, 8)), dma((2,)), dma((2, 8)),
            dma((2,)), dma((2, 4)),
            dma((4,)), dma((2, 4)), dma((3,)),
            dma((n_steps,)), dma((n_steps,)), dma((2,)),
        ],
        compiler_params=pltpu.CompilerParams(
            collective_id=0, has_side_effects=True, vmem_limit_bytes=64 * 1024 * 1024 - 65536
        ),
        name="block",
    )(
        tokens, cotangent, lengths, w_qkv.transpose(1, 0, 2), w_out.transpose(1, 0, 2), w_fc, w_proj, tab,
        b_qkv, b_fc[None], b_out[None], b_proj[None],
        gain_attn[None], shift_attn[None], gain_mlp[None], shift_mlp[None],
    )
    output, grad_tokens, g_qkv, g_out, g_fc, g_proj = res[:6]
    gain_a, shift_a, gain_m, shift_m, bias, bias_qkv, bias_fc = res[6:13]
    return (
        output,
        grad_tokens,
        g_qkv.transpose(1, 0, 2).astype(F32),
        bias_qkv,
        g_out.transpose(1, 0, 2).astype(F32),
        bias[0],
        g_fc.astype(F32),
        bias_fc[0],
        g_proj.astype(F32),
        bias[0],
        gain_a[0],
        shift_a[0],
        gain_m[0],
        shift_m[0],
    )


def solution(mesh):
    n_dp, n_tensor = mesh.devices.shape
    split = Mesh(
        mesh.devices.reshape(n_dp // INNER, INNER, n_tensor), ("outer", "inner", "tensor")
    )
    dp = ("outer", "inner")
    rows = P(("outer", "inner", "tensor"), None)
    w3 = P(dp, "tensor", None)
    w2 = P(dp, "tensor")
    return jax.shard_map(
        local,
        mesh=split,
        in_specs=(
            rows, P(dp, None), w3, P("tensor", None), w3, P(), w2, P("tensor"), w2, P(),
            P(), P(), P(), P(), rows,
        ),
        out_specs=(
            rows, rows, w3, P("tensor", None), w3, P(), w2, P("tensor"), w2, P(), P(), P(), P(), P(),
        ),
        check_vma=False,
    )
```

```python
import functools
import math

import jax
import jax.numpy as jnp
import numpy as np
from jax import lax
from jax.experimental import pallas as pl
from jax.experimental.pallas import tpu as pltpu
from jax.sharding import Mesh
from jax.sharding import PartitionSpec as P

HEAD = 256
ROT = 64
INNER = 4
UNITS = 12
UNIT = 256
WHOLE = 1
F32 = jnp.float32
BF16 = jnp.bfloat16
MESH = pl.DeviceIdType.MESH
NN = (((1,), (0,)), ((), ()))
NT = (((1,), (1,)), ((), ()))
TN = (((0,), (0,)), ((), ()))


PLAN = (
    ("a2a", 0), ("a2a", 1), ("a2a", 2), ("arrive", 0), ("ownm", 0), ("a2a", 4), ("a2a", 3), ("sp1", 0),
    ("arrive", 1), ("a2a", 7), ("a2a", 5), ("ownm", 1), ("sp1", 1), ("arrive", 2), ("ln", 0, "own"), ("ownm", 2),
    ("arrive", 3), ("pb", 0, 1), ("arrive", 4), ("ownm", 3), ("ownm", 4), ("sp2", 0), ("a2a", 6), ("ln", 0, "xy"),
    ("wx", 0, 2), ("sp1", 2), ("sp2", 1), ("pb", 0, 2), ("arrive", 5), ("ownm", 5), ("sp3", 0), ("arrive", 6),
    ("arrive", 7), ("ln", 0, "dc"), ("ln", 1, "xy"), ("sp1", 3), ("wx", 1, 2), ("wx", 0, 5, 6, 7),
    ("ln", 1, "own"), ("ownm", 6), ("need", 0), ("pb", 3, 1), ("a2a", 8), ("a2a", 9), ("need", 1), ("a2a", 10),
    ("sp3", 1), ("sp2", 2), ("wx", 1, 5, 6, 7), ("ln", 1, "rest"), ("ln", 1, "dc"), ("pb", 3, 2), ("ownm", 7),
    ("sp2", 3), ("arrive", 8), ("ln", 0, "rest"), ("sp3", 2), ("a2a", 11), ("ownm", 8), ("arrive", 9), ("need", 2),
    ("arrive", 10), ("af", 2, "a"), ("ownm", 9), ("pb", 6, 1), ("arrive", 11), ("ownm", 10), ("wx", 2, 2, 5, 6, 7),
    ("sp3", 3), ("af", 2, "b"), ("wx", 3, 2, 5, 6, 7), ("E", 0, 1), ("need", 3), ("E", 0, 2), ("ab", 2, "a"),
    ("E", 0, 3), ("ab", 2, "b"), ("t2", 0), ("M2", 0), ("pb", 6, 2), ("E", 1, 1), ("need", 4), ("need", 5),
    ("E", 2, 1), ("E", 1, 2), ("t3i", 0), ("P", 1), ("E", 2, 2), ("E", 3, 1), ("ownm", 11), ("ff", 0), ("t2", 1),
    ("t3e", 0), ("M3i", 0), ("E", 4, 1), ("M2", 1), ("E", 1, 3), ("ff", 1), ("t2", 2), ("t3i", 1), ("E", 3, 2),
    ("E", 5, 1), ("M3e", 0), ("E", 4, 2), ("E", 2, 3), ("tm", 0), ("M2", 2), ("M3i", 1), ("need", 6), ("P", 2),
    ("t3e", 1), ("ff", 2), ("need", 7), ("M3e", 1), ("pb", 9, 1), ("t2", 3), ("E", 3, 3), ("t3i", 2), ("Fm", 0),
    ("ff", 3), ("te", 0), ("need", 8), ("E", 6, 1), ("t3e", 2), ("tm", 1), ("E", 5, 2), ("E", 4, 3), ("E", 7, 1),
    ("Fe", 0), ("M2", 3), ("te", 1), ("M3i", 2), ("E", 6, 2), ("Fe", 1), ("t2", 4), ("Fm", 1), ("E", 5, 3),
    ("M2", 4), ("t3i", 3), ("ff", 4), ("M3i", 3), ("t2", 5), ("pb", 9, 2), ("P", 3), ("t3i", 4), ("E", 8, 1),
    ("E", 7, 2), ("E", 6, 3), ("M3e", 2), ("need", 9), ("ff", 5), ("t3e", 3), ("M2", 5), ("E", 9, 1), ("need", 10),
    ("M3i", 4), ("tm", 2), ("ff", 6), ("M3e", 3), ("E", 8, 2), ("need", 11), ("Fm", 2), ("t3e", 4), ("t2", 6),
    ("tm", 3), ("ff", 7), ("Fm", 3), ("t3i", 5), ("A", 0, 0), ("M2", 6), ("te", 2), ("M3i", 5), ("A", 1, 0),
    ("A", 0, 2), ("t3i", 6), ("B", 0, 0), ("E", 9, 2), ("Fe", 2), ("M3e", 4), ("tm", 4), ("t3e", 5), ("t2", 7),
    ("te", 3), ("M3i", 6), ("A", 0, 1), ("Fm", 4), ("M2", 7), ("M3e", 5), ("B", 1, 0), ("Fe", 3), ("tm", 5),
    ("E", 10, 1), ("te", 4), ("B", 0, 1), ("t2", 8), ("E", 11, 1), ("Fm", 5), ("t3e", 6), ("Fe", 4), ("A", 1, 1),
    ("tm", 6), ("M2", 8), ("E", 7, 3), ("t3i", 7), ("t2", 9), ("te", 5), ("M3e", 6), ("B", 0, 2), ("t3e", 7),
    ("A", 1, 2), ("M3i", 7), ("M3e", 7), ("Fe", 5), ("t3i", 8), ("t3e", 8), ("te", 6), ("E", 10, 2), ("M2", 9),
    ("t2", 10), ("B", 1, 1), ("E", 11, 2), ("M3i", 8), ("E", 8, 3), ("Fm", 6), ("Fe", 6), ("M2", 10), ("te", 7),
    ("t3i", 9), ("B", 1, 2), ("A", 1, 3), ("E", 9, 3), ("tm", 7), ("M3e", 8), ("Fe", 7), ("te", 8), ("t2", 11),
    ("M3i", 9), ("t3e", 9), ("t3i", 10), ("Fm", 7), ("M2", 11), ("E", 10, 3), ("M3e", 9), ("M3i", 10), ("t3i", 11),
    ("tm", 8), ("t3e", 10), ("B", 1, 3), ("M3e", 10), ("vs", 0), ("t3e", 11), ("Fm", 8), ("M3i", 11), ("Fe", 8),
    ("te", 9), ("tm", 9), ("A", 0, 3), ("M3e", 11), ("vs", 1), ("E", 11, 3), ("Fe", 9), ("Fm", 9), ("te", 10),
    ("tm", 10), ("B", 0, 3), ("Fm", 10), ("vs", 2), ("Fe", 10), ("tm", 11), ("te", 11), ("C", 0), ("own", 0),
    ("Fe", 11), ("Fm", 11), ("C", 1), ("own", 1), ("vs", 3),
)


def dot(a, b, dims=NN):
    return lax.dot_general(a, b, dims, preferred_element_type=F32)


def kernel(
    n, tokens, cot, lens, wq, wo, w_fc, w_proj, tab, b_qkv, b_fc, b_out, b_proj,
    gain_attn, shift_attn, gain_mlp, shift_mlp,
    out_ref, gtok_ref, gq_ref, go_ref, gfc_ref, gpj_ref,
    s_gain_a, s_shift_a, s_gain_m, s_shift_m, s_bias, s_bqkv, s_bfc,
    xa, rbuf, fc_buf, fh_buf, fb_buf,
    W, LB, RT, HP, HB, STG, INB, FIN, XT, TAB, PAY, SV, SVR, LENB, BQ, BF,
    p_ss, p_rs, a_ss, a_rs, a_ls, g_ss, g_rs, r_ss, r_rs, r_ls, o_ss, o_rs, o_ls,
    x_ss, x_rs, x_ls, l_ls, f_ss, f_rs, h_ss, h_rs, fl, v_ss, v_rs, loc,
):
    z = lax.axis_index("outer")
    i = lax.axis_index("inner")
    y = lax.axis_index("tensor")
    rows, width = tokens.shape
    depth = STG.shape[0]
    B = width // n
    R = B // INNER
    group = 2 * rows
    groups = INNER
    ff = UNIT * 4
    ends = z // (n - 1) + (n - 1 - z) // (n - 1)
    mid = (z > 0) & (z < n - 1)
    iC = i + 1 - 2 * lax.rem(i, 2)
    iX = lax.rem(i + 2, INNER)
    iXC = INNER - 1 - i
    inner_peers = (iC, iX, iXC)
    dC, dX, dY = {"inner": iC}, {"inner": iX}, {"tensor": 1 - y}
    dD = {"inner": iX, "tensor": 1 - y}

    def ds(start, size, mult):
        return pl.ds(pl.multiple_of(start, mult), size)

    def remote(src, dst, ss, rs, dev):
        return pltpu.make_async_remote_copy(
            src_ref=src, dst_ref=dst, send_sem=ss, recv_sem=rs, device_id=dev, device_id_type=MESH
        )

    bar = pltpu.get_barrier_semaphore()
    greet = [dC, dX, dY, dD, {"inner": iXC}] + [{"outer": lax.rem(z + m, n)} for m in range(1, n)]
    for dev in greet:
        pl.semaphore_signal(bar, inc=1, device_id=dev, device_id_type=MESH)
    pl.semaphore_wait(bar, len(greet))

    def piece(u, to):
        if u < 3:
            return wq.at[to, :, pl.ds(u * UNIT, UNIT)]
        if u == 3:
            return wo.at[to]
        ref = (w_fc, w_proj)[u % 2]
        return ref.at[:, ds(to * ff + (u - 4) // 2 * UNIT, UNIT, UNIT)]

    def a2a_copy(u, p):
        dst = W.at[u, ds(z * B + i * R, R, R)]
        return remote(
            piece(u, inner_peers[p]), dst, a_ss.at[u, p], a_rs.at[u, p], {"inner": inner_peers[p]}
        )

    def a2a_own(u):
        return pltpu.make_async_copy(piece(u, i), W.at[u, ds(z * B + i * R, R, R)], a_ls.at[u])

    def a2a(*units):
        for u in units:
            for p in (1, 2, 0):
                a2a_copy(u, p).start()
            a2a_own(u).start()

    def g_copy(u, j, e, s):
        blk = W.at[u, ds(j * B, B, B)]
        return remote(blk, blk, g_ss.at[u, e, s], g_rs.at[u, j], {"outer": z + 1 - 2 * e})

    def send_own(u):
        for e in range(2):
            @pl.when((z < n - 1) if e == 0 else (z > 0))
            def _():
                g_copy(u, z, e, 0).start()

    def arrive(*units):
        for u in units:
            for p in range(3):
                a2a_copy(u, p).wait_recv()
            a2a_own(u).wait()

            @pl.when(ends > 0)
            def _():
                send_own(u)

    def own_batch(*units):
        @pl.when(mid)
        def _():
            for u in units:
                send_own(u)

    def pass_on(u, s):
        for e in range(2):
            sgn = 1 - 2 * e
            j = z - sgn * s

            @pl.when((j >= 0) & (j < n))
            def _():
                g_copy(u, j, e, s).wait_recv()

                @pl.when((z < n - 1) if e == 0 else (z > 0))
                def _():
                    g_copy(u, j, e, s).start()

    def pass_batch(first, lo, hi):
        @pl.when(mid)
        def _():
            @pl.loop(lo, hi)
            def _(s):
                @pl.loop(first, first + 3)
                def _(u):
                    pass_on(u, s)

    def need(u):
        @pl.when(ends > 0)
        def _():
            @pl.loop(1, n)
            def _(s):
                pass_on(u, s)

    def left(v):
        return 0 if v == 0 else 1 if v < 4 else v % 2 * 2

    def stage(e, s):
        return (1 - e) * (s - 1) + e * (n - 1 - s)

    def r_copy(v, e, s):
        at, k = v % depth, stage(e, s)
        return remote(
            STG.at[at, k], rbuf.at[v, e, s - 1], r_ss.at[at, k], r_rs.at[v, e, s - 1],
            {"outer": z + 1 - 2 * e},
        )

    def r_load(v, e, s):
        return pltpu.make_async_copy(rbuf.at[v, e, s - 1], INB.at[e, s - 1], r_ls.at[e, s - 1])

    def partial(v, d):
        return dot(RT[v], LB[left(v), :, ds(d * B, B, 128)])

    def send_sum(v, e, s, val):
        if v >= depth:
            r_copy(v, e, s).wait_send()
        STG[v % depth, stage(e, s)] = val.astype(BF16)
        r_copy(v, e, s).start()

    def ahead(v):
        at = pl.ds((v - 1) * B, B)

        @pl.when(mid)
        def _():
            XT[:, at] = partial(v, z + 1 - 2 * last_way(True)).astype(BF16)

        @pl.when(ends > 0)
        def _():
            INB[(v - 1) // 2, (v - 1) % 2] = partial(v, z).astype(BF16)

    def fetch(v, e, s):
        r_copy(v, e, s - 1).wait_recv()
        r_load(v, e, s - 1).start()

    def ends_send(v, k):
        lo, hi = (1, n - 2) if k == 1 else (n - 4 + k, n - 3 + k)

        @pl.when(ends > 0)
        def _():
            e = z // (n - 1)

            @pl.loop(lo, hi)
            def _(s):
                send_sum(v, e, s, partial(v, z + (1 - 2 * e) * (n - s)))

    def mid_steps(lo, hi, body):
        @pl.when(mid)
        def _():
            @pl.loop(lo, hi)
            def _(s):
                @pl.loop(0, 2)
                def _(e):
                    d = z + (1 - 2 * e) * (n - s)

                    @pl.when((d >= 0) & (d < n))
                    def _():
                        body(e, s, d)

    def mid_fetch(v, s):
        mid_steps(s, s + 1, lambda e, s, d: fetch(v, e, s))

    def add_and_send(v, e, s, d):
        r_load(v, e, s - 1).wait()
        send_sum(v, e, s, partial(v, d) + INB[e, s - 2].astype(F32))

    def mid_send(v):
        def body(e, s, d):
            if n != 4:
                fetch(v, e, s)
            add_and_send(v, e, s, d)

        mid_steps(2, n - 1, body)

    def last_way(outward):
        e = z // (n // 2)
        return 1 - e if outward else e

    def last_fetch(v, outward):
        @pl.when(mid)
        def _():
            fetch(v, last_way(outward), n - 1)

    def last_send(v, outward):
        @pl.when(mid)
        def _():
            e = last_way(outward)
            if outward and 0 < v < 4:
                r_load(v, e, n - 2).wait()
                own = XT[:, pl.ds((v - 1) * B, B)].astype(F32)
                send_sum(v, e, n - 1, own + INB[e, n - 3].astype(F32))
            else:
                add_and_send(v, e, n - 1, z + 1 - 2 * e)

    def end_fetch(v):
        @pl.when(ends > 0)
        def _():
            fetch(v, 1 - z // (n - 1), n)

    def o_copy(v, slot, p, dst):
        if p == 3:
            return pltpu.make_async_copy(FIN.at[slot, ds(i * R, R, R)], dst, o_ls.at[slot])
        src = FIN.at[slot, ds(inner_peers[p] * R, R, R)]
        return remote(src, dst, o_ss.at[slot, p], o_rs.at[v, p], {"inner": inner_peers[p]})

    def o_sent(slot):
        for p in range(3):
            o_copy(0, slot, p, go_ref.at[i]).wait_send()
        o_copy(0, slot, 3, go_ref.at[i]).wait()

    def finish(v, total):
        slot = v % 2
        if v > 1:
            o_sent(slot)
        FIN[slot] = total.T.astype(BF16)
        at = ds(i * ff + (v - 4) // 2 * UNIT, UNIT, UNIT) if v >= 4 else None
        if v == 0:
            dst = go_ref.at[i]
        elif v < 4:
            dst = gq_ref.at[i, :, pl.ds((v - 1) * UNIT, UNIT)]
        else:
            dst = (gpj_ref, gfc_ref)[v % 2].at[:, at]
        for p in (1, 2, 0, 3):
            o_copy(v, slot, p, dst).start()

    def mid_finish(v):
        @pl.when(mid)
        def _():
            for e in range(2):
                r_load(v, e, n - 1).wait()
            finish(v, partial(v, z) + INB[0, n - 2].astype(F32) + INB[1, n - 2].astype(F32))

    def end_finish(v):
        @pl.when(ends > 0)
        def _():
            e = 1 - z // (n - 1)
            r_load(v, e, n - 1).wait()
            own = INB[(v - 1) // 2, (v - 1) % 2].astype(F32) if 0 < v < 4 else partial(v, z)
            finish(v, own + INB[e, n - 2].astype(F32))

    def block_of(fx, fy, fc):
        at = lax.rem(i + 2 * fx, INNER)
        at = at + fc * (1 - 2 * lax.rem(at, 2))
        return at * 2 + lax.rem(y + fy, 2)

    def block_rows(k):
        return block_of(lax.rem(k, 2), lax.rem(k // 2, 2), k // 4)

    half = rows // 2

    def part(ref, b, which=None):
        if which is None:
            return ref.at[ds(b * rows, rows, rows)]
        return ref.at[ds(b * rows + which * half, half, half)]

    own_b, x_b, y_b, d_b = (block_of(a, b, 0) for a, b in ((0, 0), (1, 0), (0, 1), (1, 1)))

    def x_sends(a, h, src, dst):
        def mk(k, s, d, dev):
            return remote(s, d, x_ss.at[a, k], x_rs.at[a, k], dev)

        way, on = ((dY, x_b), (dX, y_b))[a == 1]
        return [
            mk(0, src, part(dst, own_b, h), dX),
            mk(1, src, part(dst, own_b, h), dY),
            mk(2, src, part(dst, own_b, h), dC),
            mk(3, part(dst, on, h), part(dst, on, h), way),
            None,
            mk(5, part(dst, x_b, h), part(dst, x_b, h), dC),
            mk(6, part(dst, y_b, h), part(dst, y_b, h), dC),
            mk(7, part(dst, d_b, h), part(dst, d_b, h), dC),
        ]

    gb_ref = LB.at[0]
    xs = [x_sends(h, h, tokens.at[pl.ds(h * half, half)], xa) for h in range(2)]
    xs += [x_sends(2 + h, h, part(gb_ref, own_b, h), gb_ref) for h in range(2)]
    x_local = pltpu.make_async_copy(tokens, part(xa, own_b), x_ls.at[0])
    c_local = pltpu.make_async_copy(cot, part(gb_ref, own_b), x_ls.at[1])

    def near(h, k, src=None):
        b = block_rows(k)
        return pltpu.make_async_copy(
            part(xa, b, h) if src is None else src.at[pl.ds(h * half, half)], part(LB.at[2], b, h), l_ls.at[h, k]
        )

    def spread_first(a):
        for k in (1, 0, 2):
            xs[a][k].start()

    def spread_second(a):
        for k in (1, 0) if a == 1 else (0, 1):
            xs[a][k].wait_recv()
            if k == (a == 1):
                xs[a][3].start()
            xs[a][5 + k].start()

    def spread_third(a):
        xs[a][3].wait_recv()
        xs[a][7].start()

    def stats(v):
        center = v - jnp.mean(v, axis=-1, keepdims=True)
        inv = lax.rsqrt(jnp.mean(center * center, axis=-1, keepdims=True) + 1e-05)
        return center * inv, inv

    def norm_block(h, k):
        b = block_rows(k)
        near(h, k).wait()

        @pl.loop(0, half // 16, unroll=2)
        def _(t):
            to = ds(b * rows + h * half + t * 16, 16, 16)
            hat, _ = stats(LB[2, to].astype(F32))
            LB[1, to] = (hat * gain_attn[...] + shift_attn[...]).astype(BF16)
            LB[2, to] = (hat * gain_mlp[...] + shift_mlp[...]).astype(BF16)

    def p_copy(p):
        return remote(PAY, LENB.at[i], p_ss.at[p], p_rs.at[p], {"inner": inner_peers[p]})

    tab_in = pltpu.make_async_copy(tab, TAB, loc.at[0])
    p_own = pltpu.make_async_copy(PAY, LENB.at[i], loc.at[1])
    first = lens[0, 0]
    both = first + lens[0, 1]
    own_at = y * rows + lax.broadcasted_iota(jnp.int32, (16, 1), 0)

    def lengths_out():
        x_local.start()
        for h in range(2):
            near(h, 0, tokens).start()
        c_local.start()
        BQ[...] = jnp.zeros_like(BQ)
        BF[...] = jnp.zeros_like(BF)
        SV[...] = jnp.zeros_like(SV)
        tab_in.wait()
        for k, at in enumerate((first, both)):
            for h in range(2):
                PAY[2 * k + h : 2 * k + h + 1] = TAB[h, pl.ds(at, 1)]
            PAY[4 + k : 5 + k] = jnp.full((1, 128), at.astype(F32))
        PAY[6:8] = jnp.zeros((2, 128), F32)
        for p in range(3):
            p_copy(p).start()
        p_own.start()

    def lengths_in():
        for p in range(3):
            p_copy(p).wait_recv()
        p_own.wait()

    def rows_out(a):
        if a == 2:
            c_local.wait()

            @pl.loop(0, rows // 16)
            def _(t):
                to = ds(own_b * rows + t * 16, 16, 16)
                live = own_at + t * 16 < both
                LB[0, to] = jnp.where(live, LB[0, to].astype(F32), 0.0).astype(BF16)

        spread_first(a)

    def rows_on(a):
        spread_second(a)
        if a < 2:
            near(a, 1).start()
            near(a, 2).start()

    def rows_last(a):
        spread_third(a)
        if a < 2:
            near(a, 3).start()

    def rows_in(a, *ks):
        for k in ks:
            xs[a][k].wait_recv()
            if a < 2:
                near(a, {2: 4}.get(k, k)).start()
        if a == 0 and ks[0] == 2:
            x_local.wait()

    def norms(h, which):
        for k in {"own": (0,), "xy": (1, 2), "dc": (3, 4)}.get(which, ()):
            norm_block(h, k)
        if which == "rest":
            @pl.loop(5, 8)
            def _(k):
                norm_block(h, k)

    scale = 1.0 / math.sqrt(HEAD)
    lane = lax.broadcasted_iota(jnp.int32, (group, 128), 1)
    row_at = lax.broadcasted_iota(jnp.int32, (group, 1), 0).astype(F32)
    q_at = lax.broadcasted_iota(jnp.int32, (group, group), 0)
    k_at = lax.broadcasted_iota(jnp.int32, (group, group), 1)

    def turning(g):
        info = LENB[g]
        a, ab = info[4:5, 0:1], info[5:6, 0:1]
        in_a = row_at < a
        in_b = row_at < ab
        ca = jnp.where(in_a, 1.0, jnp.where(in_b, info[0:1], info[2:3]))
        sa = jnp.where(in_a, 0.0, jnp.where(in_b, info[1:2], info[3:4]))
        tcos, tsin = TAB[0, :group], TAB[1, :group]
        cosine = tcos * ca + tsin * sa
        sine = tsin * ca - tcos * sa
        low = jnp.where(lane < ROT // 2, -sine, 0.0)
        high = jnp.where(lane < ROT // 2, 0.0, sine)
        begin = jnp.where(in_a, 0.0, jnp.where(in_b, a, ab)).astype(jnp.int32)
        return cosine, low, high, begin

    def turn(v, cosine, low, high):
        first = v[:, :128]
        first = (
            first * cosine
            + pltpu.roll(first, 128 - ROT // 2, 1) * low
            + pltpu.roll(first, ROT // 2, 1) * high
        )
        return jnp.concatenate([first, v[:, 128:]], axis=1)

    def keep(slot, g, v):
        for h in range(group // 256):
            RT[slot, :, ds(g * group + h * 256, 256, 256)] = v[h * 256 : (h + 1) * 256]

    def kept(slot, g):
        return jnp.concatenate(
            [RT[slot, :, ds(g * group + h * 256, 256, 256)] for h in range(group // 256)], axis=0
        )

    def softmax(q, kk, begin):
        scores = dot(q, kk, NT) * scale
        allowed = (k_at <= q_at) & (k_at >= begin)
        scores = jnp.where(allowed, scores, -1e30)
        shifted = jnp.exp(scores - jnp.max(scores, axis=-1, keepdims=True))
        return shifted / jnp.sum(shifted, axis=-1, keepdims=True)

    def attend(lo, hi):
        @pl.loop(lo, hi)
        def _(g):
            at = ds(g * group, group, group)
            cosine, low, high, begin = turning(g)
            nm = LB[1, at]
            bias = [b_qkv[pl.ds(i, 1), r * UNIT : (r + 1) * UNIT] for r in range(3)]
            q = turn(dot(nm, W[0]) + bias[0], cosine, low, high).astype(BF16)
            keep(4, g, q)
            kk = turn(dot(nm, W[1]) + bias[1], cosine, low, high).astype(BF16)
            keep(5, g, kk)
            vv = (dot(nm, W[2]) + bias[2]).astype(BF16)
            keep(6, g, vv)
            probs = softmax(q, kk, begin).astype(BF16)
            mixed = dot(probs, vv).astype(BF16)
            RT[0, :, at] = mixed.T

    def attend_back(lo, hi):
        @pl.loop(lo, hi)
        def _(g):
            at = ds(g * group, group, group)
            cosine, low, high, begin = turning(g)
            q, kk, vv = kept(4, g), kept(5, g), kept(6, g)
            probs = softmax(q, kk, begin)
            gm = dot(LB[0, at], W[3]).astype(BF16)
            gp = dot(gm, vv, NT)
            gs = (probs * (gp - jnp.sum(probs * gp, axis=-1, keepdims=True))).astype(BF16)
            gv = dot(probs.astype(BF16), gm, TN).astype(BF16)
            gq = turn(dot(gs, kk) * scale, cosine, -low, -high).astype(BF16)
            gk = turn(dot(gs, q, TN) * scale, cosine, -low, -high).astype(BF16)
            for r, val in enumerate((gq, gk, gv)):
                RT[1 + r, :, at] = val.T
                BQ[r : r + 1] += jnp.sum(val.astype(F32), axis=0, keepdims=True)

    def hidden_of(c):
        u = 4 + 2 * c

        @pl.loop(0, groups, unroll=2 if n == 4 else 1)
        def _(g):
            at = ds(g * group, group, group)
            pre = dot(LB[2, at], W[u]) + b_fc[:, ds(i * ff + c * UNIT, UNIT, UNIT)]
            phi = 0.5 * (1.0 + lax.erf(pre * (1.0 / math.sqrt(2.0))))
            slope = phi + pre * jnp.exp(-0.5 * pre * pre) * (1.0 / math.sqrt(2.0 * math.pi))
            for h in range(group // 256):
                HP[:, ds(g * group + h * 256, 256, 256)] = slope[h * 256 : (h + 1) * 256]
            RT[u, :, at] = (pre * phi).astype(BF16).T

    def grad_of(c):
        u = 4 + 2 * c

        @pl.loop(0, groups, unroll=2 if n == 4 else 1)
        def _(g):
            at = ds(g * group, group, group)
            gh = dot(LB[0, at], W[u + 1])
            slope = jnp.concatenate(
                [HP[:, ds(g * group + h * 256, 256, 256)] for h in range(group // 256)], axis=0
            )
            val = (gh * slope).astype(BF16)
            BF[c] += jnp.sum(val.astype(F32), axis=0, keepdims=True)
            RT[u + 1, :, at] = val.T

    FS = LB.at[1]
    wide = 512
    tiles = width // wide

    def slot(k):
        return FS.at[pl.ds(k * rows, rows)]

    LT = FS.at[pl.ds(7 * rows, rows)]

    def side(us, to):
        return jnp.concatenate([W[u, to] for u in us], axis=1)

    def turn_left(b, vs):
        at = ds(b * rows, rows, rows)
        for k, v in enumerate(vs):
            LT[:, k * UNIT : (k + 1) * UNIT] = RT[v, :, at].T

    def branch_block(b):
        turn_left(b, (0, 4, 6, 8, 10))

        @pl.loop(0, tiles)
        def _(t):
            to = ds(t * wide, wide, wide)
            HB[:, to] = dot(LT[:, : 5 * UNIT], side((3, 5, 7, 9, 11), to), NT)

    def x_block(b):
        return pltpu.make_async_copy(part(xa, b), XT, loc.at[0])

    def input_block(b):
        x_block(b).start()
        turn_left(b, (1, 2, 3, 5, 7, 9, 11))
        x_block(b).wait()
        v = XT[...].astype(F32)
        mean = jnp.mean(v, axis=-1, keepdims=True)
        center = v - mean
        inv = lax.rsqrt(jnp.mean(center * center, axis=-1, keepdims=True) + 1e-05)

        @pl.loop(0, tiles)
        def _(t):
            to = ds(t * wide, wide, wide)
            na = dot(LT[:, : 3 * UNIT], side((0, 1, 2), to), NT)
            nm = dot(LT[:, 3 * UNIT : 7 * UNIT], side((4, 6, 8, 10), to), NT)
            hat = (XT[:, to].astype(F32) - mean) * inv
            SV[0:1, to] += jnp.sum(na * hat, axis=0, keepdims=True)
            SV[1:2, to] += jnp.sum(na, axis=0, keepdims=True)
            SV[2:3, to] += jnp.sum(nm * hat, axis=0, keepdims=True)
            SV[3:4, to] += jnp.sum(nm, axis=0, keepdims=True)
            HP[:, to] = na * gain_attn[:, to] + nm * gain_mlp[:, to]

    blocks = (branch_block, input_block)
    totals = (HB, HP)

    def c_copy(a, k):
        return remote(slot(k % 2), fc_buf.at[a, k], f_ss.at[k % 2], f_rs.at[a, k], dC)

    sent = []

    def fold_over(a, k):
        blocks[a](block_of((3 - k) // 2, (3 - k) % 2, 1))
        for op in [op for op in sent if op[0] == k % 2]:
            op[1].wait_send()
            sent.remove(op)
        slot(k % 2)[...] = totals[a][...].astype(BF16)
        op = c_copy(a, k)
        op.start()
        sent.append((k % 2, op))

    def h_copy(a, w):
        if w > 1:
            src, dst = slot(1 + w), fb_buf.at[a, w - 2]
        elif a == WHOLE:
            src, dst = slot(2), fh_buf.at[a]
        else:
            src, dst = FS.at[pl.ds(2 * rows + w * half, half)], fh_buf.at[a, pl.ds(w * half, half)]
        return remote(src, dst, h_ss.at[w], h_rs.at[a, w], (dX, dY)[w % 2])

    going = {}

    def fold_own(a, k):
        c_copy(a, k).wait_recv()
        get = pltpu.make_async_copy(fc_buf.at[a, k], slot(5), fl.at[0])
        get.start()
        extra = None
        size = rows if a == WHOLE else half
        at = pl.ds(0, rows) if a == WHOLE else pl.ds(half, half) if k == 1 else pl.ds(0, half)
        if k == 1 or (k == 2 and a != WHOLE):
            h_copy(a, 2 - k).wait_recv()
            extra = pltpu.make_async_copy(fh_buf.at[a, at], FS.at[pl.ds(6 * rows, size)], fl.at[1])
            extra.start()
        blocks[a](block_of((3 - k) // 2, (3 - k) % 2, 0))
        get.wait()
        if extra is not None:
            extra.wait()
            totals[a][at] += FS[pl.ds(6 * rows, size)].astype(F32)
        if k < 3:
            for w in ((0, 1), (2,), (3,))[k]:
                if w in going:
                    going.pop(w).wait_send()
            slot(2 + k)[...] = (totals[a][...] + slot(5)[...].astype(F32)).astype(BF16)
            for w in ((1,) if a == WHOLE else (0, 1), (2,), (3,))[k]:
                going[w] = h_copy(a, w)
                going[w].start()
        else:
            totals[a][...] += slot(5)[...].astype(F32)

    def fold_end(a):
        gets = [pltpu.make_async_copy(fb_buf.at[a, j], slot(5 + j), fl.at[j]) for j in range(2)]
        for j in range(2):
            h_copy(a, 2 + j).wait_recv()
            gets[j].start()
        for get in gets:
            get.wait()

    def own_tiles(a, to_ref, base, body):
        @pl.loop(0, rows // 16, unroll=2)
        def _(t):
            at = ds(t * 16, 16, 16)
            u = (
                totals[a][at]
                + FS[ds(5 * rows + t * 16, 16, 16)].astype(F32)
                + FS[ds(6 * rows + t * 16, 16, 16)].astype(F32)
            )
            to_ref[ds(base + t * 16, 16, 16)] = body(t, at, u).astype(BF16)

    keep_row = lax.broadcasted_iota(jnp.int32, (16, 1), 0) < 5
    chip = (i // 2) * 2 + y

    def v_copies(k):
        if k == 0:
            return [(dC, 0, 0)]
        if k == 1:
            return [(dev, 1 + m, 1 + chip) for m, dev in enumerate((dX, dY, dD))]
        return [({"outer": lax.rem(z + m, n)}, 3 + m, 5 + z) for m in range(1, n)] if n == 4 else []

    def v_copy(dev, at, to):
        return remote(SV, SVR.at[to], v_ss.at[at], v_rs.at[to], dev)

    def v_start(k):
        if k == 1:
            SVR[1 + chip] = SV[...]
        if k == 2 and n == 4:
            SVR[5 + z] = SV[...]
        for args in v_copies(k):
            v_copy(*args).start()

    def v_wait(k):
        for args in v_copies(k):
            v_copy(*args).wait_send()
        if k == 0:
            v_copy(dC, 0, 0).wait_recv()
        if k == 1:
            for m, at in enumerate(((i // 2 + 1) % 2 * 2 + y, i // 2 * 2 + 1 - y, (i // 2 + 1) % 2 * 2 + 1 - y)):
                v_copy(dX, 1 + m, 1 + at).wait_recv()
        if k == 2 and n == 4:
            for m in range(1, n):
                v_copy(dX, 3 + m, 5 + lax.rem(z + m, n)).wait_recv()

    def small_sums(k):
        if k == 0:
            SV[4:5] = jnp.sum(LB[0, ds(own_b * rows, rows, rows)].astype(F32), axis=0, keepdims=True)
            for r in range(3):
                SV[pl.ds(5 + i, 1), r * UNIT : (r + 1) * UNIT] = BQ[r : r + 1]
            for c in range(4):
                SV[pl.ds(5 + i, 1), (3 + c) * UNIT : (4 + c) * UNIT] = BF[c]
            v_start(0)
            return
        v_wait(k - 1)
        if k == 1:
            SV[...] += SVR[0]
        elif k == 2:
            total = jnp.zeros((16, width), F32)
            for q in range(4):
                total += jnp.where(keep_row | (y == q % 2), SVR[1 + q], 0.0)
            SV[...] = total
        elif n != 4:
            for m in range((n - 1).bit_length()):
                other = z + 2**m * (1 - 2 * lax.rem(z // 2**m, 2))
                op = v_copy({"outer": other}, 3 + m, 5 + m)
                op.start()
                op.wait()
                SV[...] += SVR[5 + m]
        else:
            total = SVR[5]
            for q in range(1, n):
                total += SVR[5 + q]
            SV[...] = total
        if k < 3:
            v_start(k)
            return
        s_gain_a[...] = SV[0:1]
        s_shift_a[...] = SV[1:2]
        s_gain_m[...] = SV[2:3]
        s_shift_m[...] = SV[3:4]
        s_bias[...] = SV[4:5]
        s_bqkv[...] = SV[5 : 5 + INNER, : 3 * UNIT]
        for j in range(INNER):
            s_bfc[:, j * ff : (j + 1) * ff] = SV[5 + j : 6 + j, 3 * UNIT : 3 * UNIT + ff]

    def own_out():
        x_block(own_b).start()
        x_block(own_b).wait()
        bias = b_out[...] + b_proj[...]

        def body(t, at, u):
            live = (own_at + t * 16 < both).astype(F32)
            return XT[at].astype(F32) + live * (u + bias)

        own_tiles(0, XT, 0, body)
        put_out.start()

    def own_grad():
        put_out.wait()
        x_block(own_b).start()
        for w in list(going):
            going.pop(w).wait_send()
        get = pltpu.make_async_copy(cot, slot(4), fl.at[2])
        get.start()
        x_block(own_b).wait()
        get.wait()

        def body(t, at, u):
            hat, inv = stats(XT[at].astype(F32))
            return FS[ds(4 * rows + t * 16, 16, 16)].astype(F32) + inv * (
                u - jnp.mean(u, axis=-1, keepdims=True) - hat * jnp.mean(u * hat, axis=-1, keepdims=True)
            )

        own_tiles(1, FS, 7 * rows, body)
        put_grad.start()

    put_out = pltpu.make_async_copy(XT, out_ref, fl.at[2])
    put_grad = pltpu.make_async_copy(slot(7), gtok_ref, fl.at[2])

    def own_rows(a):
        (own_out, own_grad)[a]()

    def ff_half(r):
        (hidden_of, grad_of)[r % 2](r // 2)

    ops = {
        "a2a": a2a,
        "arrive": arrive,
        "ownm": own_batch,
        "pb": lambda f, s: pass_batch(f, 1, 2) if s == 1 else pass_batch(f, 2, n - 1),
        "need": need,
        "sp1": rows_out,
        "sp2": rows_on,
        "sp3": rows_last,
        "wx": rows_in,
        "ln": norms,
        "af": lambda c, h: attend(*((0, groups // 2) if h == "a" else (groups // 2, groups))),
        "ab": lambda c, h: attend_back(*((0, groups // 2) if h == "a" else (groups // 2, groups))),
        "ff": ff_half,
        "P": ahead,
        "E": ends_send,
        "t2": lambda v: mid_fetch(v, 2) if n == 4 else None,
        "M2": mid_send,
        "t3i": lambda v: last_fetch(v, False),
        "t3e": lambda v: last_fetch(v, True),
        "M3i": lambda v: last_send(v, False),
        "M3e": lambda v: last_send(v, True),
        "tm": lambda v: mid_fetch(v, n),
        "Fm": mid_finish,
        "te": end_fetch,
        "Fe": end_finish,
        "A": fold_over,
        "B": fold_own,
        "C": fold_end,
        "own": own_rows,
        "vs": small_sums,
    }
    tab_in.start()
    for op in PLAN:
        if op == ("af", 2, "a"):
            lengths_in()
        ops[op[0]](*op[1:])
        if op == ("sp1", 0):
            lengths_out()
    put_grad.wait()

    for p in range(3):
        p_copy(p).wait_send()

    @pl.loop(0, UNITS)
    def _(u):
        for p in range(3):
            o_copy(u, 0, p, go_ref.at[i]).wait_recv()

    for u in range(UNITS):
        for p in range(3):
            a2a_copy(u, p).wait_send()
    for op in sum(xs, []):
        if op is not None:
            op.wait_send()

    @pl.loop(0, UNITS)
    def _(u):
        for e in range(2):
            sgn = 1 - 2 * e

            @pl.when((z < n - 1) if e == 0 else (z > 0))
            def _():
                @pl.loop(0, n)
                def _(s):
                    j = z - sgn * s

                    @pl.when((j >= 0) & (j < n))
                    def _():
                        g_copy(u, j, e, s).wait_send()

    for e in range(2):
        @pl.loop(1, n)
        def _(s):
            d = z + (1 - 2 * e) * (n - s)

            @pl.when((d >= 0) & (d < n))
            def _():
                for k in range(depth):
                    r_copy(UNITS - 1 - k, e, s).wait_send()

    for s in range(2):
        o_sent(s)
    for _, op in sent:
        op.wait_send()


def local(
    tokens, lengths, w_qkv, b_qkv, w_out, b_out, w_fc, b_fc, w_proj, b_proj,
    gain_attn, shift_attn, gain_mlp, shift_mlp, cotangent,
):
    n = lax.axis_size("outer")
    rows, width = tokens.shape
    R = w_qkv.shape[0]
    B = INNER * R
    group = rows * lax.axis_size("tensor")

    lane = np.arange(128)
    freq = np.where(lane < ROT, np.exp((lane % (ROT // 2)) * (2.0 / ROT) * -math.log(10000.0)), 0.0)
    angle = np.arange(group + 8, dtype=np.float32)[:, None] * freq.astype(np.float32)
    tab = jnp.asarray(np.stack([np.cos(angle), np.sin(angle)]).astype(np.float32))

    tall = INNER * group
    depth = 2 if n == 4 else 1
    logn = (n - 1).bit_length()
    hbm = pl.BlockSpec(memory_space=pl.ANY)
    vmem = pl.BlockSpec(memory_space=pltpu.VMEM)
    smem = pl.BlockSpec(memory_space=pltpu.SMEM)
    sds = jax.ShapeDtypeStruct
    dma = pltpu.SemaphoreType.DMA
    row = sds((1, width), F32)
    res = pl.pallas_call(
        functools.partial(kernel, n),
        out_shape=(
            sds((rows, width), BF16),
            sds((rows, width), BF16),
            sds((INNER, R, 3 * UNIT), BF16),
            sds((INNER, R, UNIT), BF16),
            sds(w_fc.shape, BF16),
            sds(w_proj.shape, BF16),
            row, row, row, row, row,
            sds(b_qkv.shape, F32),
            sds((1,) + b_fc.shape, F32),
            sds((tall, width), BF16),
            sds((UNITS, 2, n - 1, UNIT, B), BF16),
            sds((2, 4, rows, width), BF16),
            sds((2, rows, width), BF16),
            sds((2, 2, rows, width), BF16),
        ),
        in_specs=[hbm] * 2 + [smem] + [hbm] * 5 + [vmem] * 8,
        out_specs=(hbm,) * 6 + (vmem,) * 7 + (hbm,) * 5,
        scratch_shapes=[
            pltpu.VMEM((UNITS, width, UNIT), BF16),
            pltpu.VMEM((3, tall, width), BF16),
            pltpu.VMEM((UNITS, UNIT, tall), BF16),
            pltpu.VMEM((UNIT, tall), F32),
            pltpu.VMEM((rows, width), F32),
            pltpu.VMEM((depth, n - 1, UNIT, B), BF16),
            pltpu.VMEM((2, n - 1, UNIT, B), BF16),
            pltpu.VMEM((2, B, UNIT), BF16),
            pltpu.VMEM((rows, width), BF16),
            pltpu.VMEM(tab.shape, F32),
            pltpu.VMEM((8, 128), F32),
            pltpu.VMEM((16, width), F32),
            pltpu.VMEM((5 + (n if n == 4 else logn), 16, width), F32),
            pltpu.VMEM((INNER, 8, 128), F32),
            pltpu.VMEM((8, UNIT), F32),
            pltpu.VMEM((4, 1, UNIT), F32),
            dma((3,)), dma((3,)),
            dma((UNITS, 3)), dma((UNITS, 3)), dma((UNITS,)),
            dma((UNITS, 2, n)), dma((UNITS, n)),
            dma((depth, n - 1)), dma((UNITS, 2, n - 1)), dma((2, n - 1)),
            dma((2, 3)), dma((UNITS, 3)), dma((2,)),
            dma((4, 8)), dma((4, 8)), dma((2,)), dma((2, 8)),
            dma((2,)), dma((2, 4)),
            dma((4,)), dma((2, 4)), dma((3,)),
            dma((3 + n,)), dma((5 + n,)), dma((2,)),
        ],
        compiler_params=pltpu.CompilerParams(
            collective_id=0, has_side_effects=True, vmem_limit_bytes=64 * 1024 * 1024 - 65536
        ),
        name="block",
    )(
        tokens, cotangent, lengths, w_qkv.transpose(1, 0, 2), w_out.transpose(1, 0, 2), w_fc, w_proj, tab,
        b_qkv, b_fc[None], b_out[None], b_proj[None],
        gain_attn[None], shift_attn[None], gain_mlp[None], shift_mlp[None],
    )
    output, grad_tokens, g_qkv, g_out, g_fc, g_proj = res[:6]
    gain_a, shift_a, gain_m, shift_m, bias, bias_qkv, bias_fc = res[6:13]
    return (
        output,
        grad_tokens,
        g_qkv.transpose(1, 0, 2).astype(F32),
        bias_qkv,
        g_out.transpose(1, 0, 2).astype(F32),
        bias[0],
        g_fc.astype(F32),
        bias_fc[0],
        g_proj.astype(F32),
        bias[0],
        gain_a[0],
        shift_a[0],
        gain_m[0],
        shift_m[0],
    )


def solution(mesh):
    n_dp, n_tensor = mesh.devices.shape
    split = Mesh(
        mesh.devices.reshape(n_dp // INNER, INNER, n_tensor), ("outer", "inner", "tensor")
    )
    dp = ("outer", "inner")
    rows = P(("outer", "inner", "tensor"), None)
    w3 = P(dp, "tensor", None)
    w2 = P(dp, "tensor")
    return jax.shard_map(
        local,
        mesh=split,
        in_specs=(
            rows, P(dp, None), w3, P("tensor", None), w3, P(), w2, P("tensor"), w2, P(),
            P(), P(), P(), P(), rows,
        ),
        out_specs=(
            rows, rows, w3, P("tensor", None), w3, P(), w2, P("tensor"), w2, P(), P(), P(), P(), P(),
        ),
        check_vma=False,
    )
```
